128 devices in a mesh: leaf: 4 (over x), grid: 32 (over z, y, core).
Axes of the slice: x: 4, y: 4, z: 4, core: 2. Of those that a mesh axis runs over, the one named last changes fastest.
Arguments:
- rhs: bfloat16 [4, 1024, 1024], P('leaf', 'grid'), may hold values from -6 to 6
- inverse_blocks: bfloat16 [4, 1024, 1024], P('leaf'), as said below
- update_blocks: bfloat16 [4, 8, 1024, 1024], P('leaf', None, 'grid'), may hold values from -0.046875 to 0.046875
- targets: int32 [4, 8, 32], P('leaf', None, 'grid'), may hold values from -1 to 3, as said below
- widths: int32 [4], P('leaf'), may hold values from 128 to 1024, as said below
Outputs:
- forward: bfloat16 [4, 1024, 1024], P('leaf', 'grid')
- solution: bfloat16 [4, 1024, 1024], P('leaf', 'grid')
The draws below stay inside these ranges and needn't reach their ends.
Inputs may be any that keep to these rules, and one draw needn't show every extreme that they name: `targets`: for supernode s every entry is -1 or a later supernode, greater than s; slot 0 is never -1 below the last supernode, all of whose entries are -1. `widths`: each is a multiple of 128; the last supernode's is 1024. `inverse_blocks`: each is lower triangular with a diagonal of positive entries.
All inputs are finite; a program needn't handle non-finite values.
Results may differ from the reference program's by a relative error of at most 0.0067.
Values may be sent and summed in bfloat16 or wider, within the bound.
A program may use at most 128 MiB of HBM per device.

```python
import math
import jax
import jax.numpy as jnp
from jax import lax

W = 1024
RHS = 1024
U_DEV = 8
SUPERNODES = 4
N_GRID = 32


def draw_inverse_blocks(key, part):
    key = jax.random.fold_in(key, 37)
    key_diagonal, key_lower = jax.random.split(key)
    lower_part = jax.random.normal(key_lower, (SUPERNODES, W, W), jnp.float32) * 0.7
    diagonal = jax.random.uniform(key_diagonal, (SUPERNODES, W), jnp.float32, 0.5, 1.5)
    row_range = jnp.arange(W)[:, None]
    col_range = jnp.arange(W)[None, :]
    strict = (row_range > col_range).astype(jnp.float32)
    identity = (row_range == col_range).astype(jnp.float32)
    assembled = lower_part * strict[None] / math.sqrt(W) + identity[None] * diagonal[:, :, None]
    return assembled.astype(jnp.bfloat16)


def draw_targets(key, part):
    key = jax.random.fold_in(key, 11)
    key_target, key_vacant = jax.random.split(key)
    shape_all = (SUPERNODES, U_DEV, N_GRID)
    source_node = jnp.arange(SUPERNODES, dtype=jnp.int32)[:, None, None]
    later_count = jnp.maximum(SUPERNODES - 1 - source_node, 1)
    drawn = jax.random.randint(key_target, shape_all, 0, 1 << 20)
    chosen = source_node + 1 + drawn % later_count
    vacant = jax.random.randint(key_vacant, shape_all, 0, 4) == 0
    slot_ids = jnp.arange(U_DEV, dtype=jnp.int32)[None, :, None]
    vacant = vacant & (slot_ids > 0) | (source_node == SUPERNODES - 1)
    return jnp.where(vacant, -1, chosen).astype(jnp.int32)


def draw_widths(key, part):
    key = jax.random.fold_in(key, 23)
    counts = jax.random.randint(key, (SUPERNODES,), 1, 9)
    counts = counts.at[SUPERNODES - 1].set(8)
    return (counts * (W // 8)).astype(jnp.int32)


def shard_levels(own_key, dims, shards, least, top_value):
    factor_of, own = 1.0, jax.random.fold_in(own_key, 6)
    for dim, parts in shards:
        heights = jnp.exp(jax.random.uniform(jax.random.fold_in(own, dim), (parts,), jnp.float32, least / len(shards), top_value / len(shards)))
        factor_of = factor_of * jnp.repeat(heights, dims[dim] // parts).reshape([-1 if axis == dim else 1 for axis in range(len(dims))])
    return factor_of


def bell_draw(own_key, extent, deviation, bound, pieces=(), held_as=jnp.bfloat16):
    factor_of = shard_levels(own_key, extent, pieces, -0.22, 0.18) if pieces else 1.0
    entries = jax.random.normal(own_key, extent, jnp.float32) * deviation * factor_of
    return jnp.minimum(jnp.maximum(entries, -bound), bound).astype(held_as)


def setup_inputs(seed: int = 0) -> dict:
    splits = jax.random.split(jax.random.key(seed), 6)
    return {
        "rhs": bell_draw(splits[0], (SUPERNODES, W, RHS), 1.0, 6.0, ((0, 4), (1, 32))),
        "inverse_blocks": draw_inverse_blocks(jax.random.fold_in(splits[5], 71), 0),
        "update_blocks": bell_draw(splits[2], (SUPERNODES, U_DEV, W, W), (2 * W * U_DEV) ** -0.5, 0.046875, ((0, 4), (2, 32))),
        "targets": draw_targets(jax.random.fold_in(splits[5], 71), 0),
        "widths": draw_widths(jax.random.fold_in(splits[5], 71), 0),
    }


def routing(targets, node_id):
    row_target = jnp.repeat(targets[node_id], W // N_GRID, axis=1)
    node_range = jnp.arange(SUPERNODES, dtype=jnp.int32)
    return (row_target[:, :, None] == node_range[None, None, :]).astype(jnp.float32)


def reference(rhs, inverse_blocks, update_blocks, targets, widths):
    row_range = jnp.arange(W, dtype=jnp.int32)
    pending = jnp.zeros((SUPERNODES, W, RHS), jnp.float32)
    solved_list = []
    for node_id in range(SUPERNODES):
        live = (row_range < widths[node_id])[:, None]
        corrected = jnp.where(live, rhs[node_id].astype(jnp.float32) - pending[node_id], 0.0).astype(jnp.bfloat16)
        solved = jnp.where(live, jnp.dot(inverse_blocks[node_id], corrected, preferred_element_type=jnp.float32), 0.0).astype(jnp.bfloat16)
        flat_blocks = update_blocks[node_id].reshape(U_DEV * W, W)
        products = jnp.dot(flat_blocks, solved, preferred_element_type=jnp.float32).reshape(U_DEV, W, RHS)
        pending = pending + jnp.einsum("urs,urk->srk", routing(targets, node_id), products, precision=lax.Precision.HIGHEST)
        solved_list.append(solved)
    forward = jnp.stack(solved_list)
    known = jnp.zeros((SUPERNODES, W, RHS), jnp.bfloat16)
    for node_id in reversed(range(SUPERNODES)):
        live = (row_range < widths[node_id])[:, None]
        gathered = jnp.einsum("urs,srk->urk", routing(targets, node_id), known.astype(jnp.float32), precision=lax.Precision.HIGHEST).astype(jnp.bfloat16)
        flat_blocks = update_blocks[node_id].reshape(U_DEV * W, W)
        coupled = jnp.dot(flat_blocks.T, gathered.reshape(U_DEV * W, RHS), preferred_element_type=jnp.float32)
        weighted = jnp.where(live, forward[node_id].astype(jnp.float32) - coupled, 0.0).astype(jnp.bfloat16)
        result = jnp.where(live, jnp.dot(inverse_blocks[node_id].T, weighted, preferred_element_type=jnp.float32), 0.0).astype(jnp.bfloat16)
        known = known.at[node_id].set(result)
    return (forward, known)
```

```python
import jax
import jax.numpy as jnp
from jax import lax
from jax.experimental import pallas as pl
from jax.experimental.pallas import tpu as pltpu
from jax.sharding import PartitionSpec as P

MESH = pl.DeviceIdType.MESH
W = 1024
PIECE = 32
GRID = 32
LINE = 4
SLOTS = 8
HALF = W // 2
NEAR = (0, -1, 1, 2)
F32 = jnp.float32
BF16 = jnp.bfloat16


def product(a, b, transposed=False):
    dims = (((1,), (1 if transposed else 0,)), ((), ()))
    return lax.dot_general(a, b, dims, preferred_element_type=F32)


def kernel(
    rhs_h, inv_h, upd_h, tgt_s, wid_s, fwd_o, sol_o,
    rhs_v, inv_v, upd_v, mats, rbuf, fbuf, obuf, wide, fsend, osend,
    part_out, part_in, state,
    in_sem, gat_send, gat_recv, all_send, all_recv, hop_send, hop_recv,
):
    leaf = lax.axis_index("leaf")
    g = lax.axis_index("grid")
    z, y, c = g // 8, (g // 2) % LINE, g % 2
    place = (z, y)

    def device(x, zz, yy, cc):
        return (x, ((zz % LINE) * LINE + (yy % LINE)) * 2 + cc)

    loads = [
        pltpu.make_async_copy(upd_h, upd_v, in_sem.at[0]),
        pltpu.make_async_copy(inv_h, inv_v, in_sem.at[1]),
        pltpu.make_async_copy(rhs_h, rhs_v, in_sem.at[2]),
    ]
    for load in loads:
        load.start()

    barrier = pltpu.get_barrier_semaphore()

    def greet(d, carry):
        pl.semaphore_signal(barrier, inc=1, device_id=(leaf, (g + d) % GRID), device_id_type=MESH)
        return carry

    lax.fori_loop(1, GRID, greet, 0)
    for d in (1, 2, 3):
        pl.semaphore_signal(barrier, inc=1, device_id=((leaf + d) % 4, g), device_id_type=MESH)

    width = wid_s[0]

    def live(rows):
        return lax.broadcasted_iota(jnp.int32, (rows, W), 1) < width

    loads[0].wait()
    rows = []
    for t in (leaf + 1, 3, 2):
        total = jnp.zeros((PIECE, W), F32)
        for u in range(SLOTS):
            total = total + jnp.where(tgt_s[u] == t, 1.0, 0.0) * upd_v[u].astype(F32)
        rows.append(total)
    stacked = jnp.where(live(3 * PIECE), jnp.concatenate(rows, axis=0), 0.0).astype(BF16)
    loads[1].wait()
    coupling = jnp.where(live(3 * PIECE), product(stacked, inv_v[...]), 0.0).astype(BF16)
    mats[0, z, y, c] = coupling[:PIECE]

    @pl.when(leaf != 2)
    def _():
        mats[1, z, y, c] = coupling[PIECE : 2 * PIECE]

    part_out[3] = coupling[2 * PIECE :]
    loads[2].wait()
    pl.semaphore_wait(barrier, GRID - 1 + 3)

    def block(j, h, i1, i2):
        if h == 0:
            return mats.at[j, i1 % LINE, i2 % LINE, c, :, pl.ds(0, HALF)]
        return mats.at[j, i2 % LINE, i1 % LINE, c, :, pl.ds(HALF, HALF)]

    def bundle(j, h, i2, core):
        if h == 0:
            return mats.at[j, :, i2 % LINE, core, :, pl.ds(0, HALF)]
        return mats.at[j, i2 % LINE, :, core, :, pl.ds(HALF, HALF)]

    def there(h, i1, i2, core):
        return device(leaf, i1, i2, core) if h == 0 else device(leaf, i2, i1, core)

    started = []

    def gather_copy(ref, j, h, slot, to):
        return pltpu.make_async_remote_copy(
            ref, ref, gat_send.at[j, h, slot], gat_recv.at[j, h, slot], device_id=to, device_id_type=MESH
        )

    def send(ref, j, h, slot, to):
        copy = gather_copy(ref, j, h, slot, to)
        copy.start()
        started.append(copy)

    def arrived(ref, j, h, slot):
        gather_copy(ref, j, h, slot, there(0, z, y, 1 - c)).wait_recv()

    def own(h):
        return place if h == 0 else (place[1], place[0])

    def to_sibling(j, h, slot, i2):
        p1, p2 = own(h)
        send(bundle(j, h, i2, c), j, h, slot, there(h, p1, p2, 1 - c))

    def gather_first(j):
        for i, d in enumerate((1, -1, 2)):
            for h in range(2):
                p1, p2 = own(h)
                send(block(j, h, p1, p2), j, h, i, there(h, p1 + d, p2, c))

    def gather_second(j):
        for i, k in enumerate(NEAR):
            for h in range(2):
                p1, p2 = own(h)
                ref = block(j, h, p1 + k, p2)
                if k:
                    arrived(ref, j, h, i - 1)
                for e, d in enumerate((1, -1)):
                    send(ref, j, h, 3 + 2 * i + e, there(h, p1, p2 + d, c))
        for h in range(2):
            to_sibling(j, h, 15, own(h)[1])

    def gather_third(j):
        for i, k in enumerate(NEAR):
            for h in range(2):
                p1, p2 = own(h)
                for e, d in enumerate((1, -1)):
                    ref = block(j, h, p1 + k, p2 - d)
                    arrived(ref, j, h, 3 + 2 * i + e)
                    if i % 2 == e:
                        send(ref, j, h, 11 + i, there(h, p1, p2 + d, c))
        for h in range(2):
            p2 = own(h)[1]
            to_sibling(j, h, 16, p2 - 1)
            to_sibling(j, h, 17, p2 + 1)

    def gather_last(j):
        for h in range(2):
            p1, p2 = own(h)
            for i, k in enumerate(NEAR):
                arrived(block(j, h, p1 + k, p2 + 2), j, h, 11 + i)
            to_sibling(j, h, 18, p2 + 2)

    def gather_wait(j):
        for h in range(2):
            p2 = own(h)[1]
            for slot, d in ((15, 0), (16, -1), (17, 1), (18, 2)):
                arrived(bundle(j, h, p2 + d, 1 - c), j, h, slot)

    def exchange(source, target, sem):
        def one(d, carry):
            to = (g + d) % GRID
            pltpu.make_async_remote_copy(
                source(to), target.at[g], all_send.at[sem], all_recv.at[sem], device_id=(leaf, to), device_id_type=MESH
            ).start()
            return carry

        lax.fori_loop(1, GRID, one, 0)

    def exchange_wait(target, sem):
        most = target.at[pl.ds(0, GRID - 1)]
        whole = pltpu.make_async_remote_copy(
            most, most, all_send.at[sem], all_recv.at[sem], device_id=(leaf, (g + 1) % GRID), device_id_type=MESH
        )
        whole.wait_recv()
        whole.wait_send()

    def rhs_columns(to):
        return rhs_v.at[:, pl.ds(pl.multiple_of((to // 4) * 128, 128), 128)]

    def hop(source, target, slot, x):
        return pltpu.make_async_remote_copy(
            source, target, hop_send.at[slot], hop_recv.at[slot], device_id=(x, g), device_id_type=MESH
        )

    move = hop(part_out.at[3], mats.at[1, z, y, c], 3, 2)

    gather_first(0)

    @pl.when(leaf == 0)
    def _():
        move.start()

    exchange(rhs_columns, rbuf, 0)
    rbuf[g] = rhs_v[:, pl.ds(pl.multiple_of((g // 4) * 128, 128), 128)]
    gather_second(0)
    gather_third(0)

    @pl.when(leaf == 2)
    def _():
        move.wait_recv()

    gather_first(1)
    exchange_wait(rbuf, 0)
    wide[...] = rbuf[...].reshape(W, 128).astype(F32).T
    mine = pl.ds(pl.multiple_of((g % 4) * PIECE, PIECE), PIECE)
    state[0] = wide[mine, :]
    wide[...] = jnp.zeros_like(wide)

    gather_last(0)
    gather_wait(0)

    def matrix(j):
        return mats[j].reshape(W, W)

    down = hop(part_out.at[0], part_in.at[0], 0, (leaf + 1) % 4)
    far = hop(part_out.at[1], part_in.at[1 + leaf % 2], 1 + leaf % 2, 3)
    early = hop(part_out.at[2], part_in.at[1], 8, 2)

    def solve_step():
        corrected = jnp.where(live(PIECE), state[0], 0.0).astype(BF16)
        part_out[2] = corrected

        @pl.when(leaf < 3)
        def _():
            part_out[0] = product(corrected, matrix(0), True).astype(BF16)
            down.start()

    @pl.when(leaf == 0)
    def _():
        solve_step()
        early.start()

    gather_second(1)

    @pl.when(leaf == 1)
    def _():
        down.wait_recv()
        state[0] = state[0] - part_in[0].astype(F32)
        solve_step()

    gather_third(1)
    gather_last(1)
    gather_wait(1)

    @pl.when(leaf < 2)
    def _():
        part_out[1] = product(part_out[2], matrix(1), True).astype(BF16)
        far.start()

    @pl.when(leaf == 2)
    def _():
        early.wait_recv()
        state[0] = state[0] - product(part_in[1], matrix(1), True)
        down.wait_recv()
        state[0] = state[0] - part_in[0].astype(F32)
        solve_step()

    @pl.when(leaf == 3)
    def _():
        hop(part_out.at[1], part_in.at[1], 1, 3).wait_recv()
        hop(part_out.at[1], part_in.at[2], 2, 3).wait_recv()
        state[0] = state[0] - part_in[1].astype(F32) - part_in[2].astype(F32)
        down.wait_recv()
        state[0] = state[0] - part_in[0].astype(F32)
        solve_step()

    forward = jnp.where(live(PIECE), product(part_out[2], inv_v[...], True), 0.0).astype(BF16)
    state[1] = jnp.where(live(PIECE), product(forward, inv_v[...]), 0.0)

    up = hop(part_out.at[4], part_in.at[3], 4, (leaf + 3) % 4)
    far_one = hop(part_out.at[4], part_in.at[4], 5, 1)
    far_zero = hop(part_out.at[4], part_in.at[4], 6, 0)
    side = hop(part_out.at[5], part_in.at[5], 7, 0)

    @pl.when(leaf == 3)
    def _():
        part_out[4] = state[1].astype(BF16)
        up.start()
        far_one.start()
        far_zero.start()

    def spread(piece, staged, target, sem):
        wide[mine, :] = piece.astype(F32)
        staged[...] = wide[...].T.astype(BF16).reshape(GRID, PIECE, 128)
        exchange(lambda to: staged.at[to], target, sem)
        target[g] = staged[g]

    def collect(target, out):
        for k in range(GRID // 4):
            total = target[4 * k]
            for q in range(1, 4):
                total = total + target[4 * k + q]
            out[:, k * 128 : (k + 1) * 128] = total

    spread(forward, fsend, fbuf, 1)

    for copy in started:
        copy.wait_send()

    @pl.when(leaf == 0)
    def _():
        move.wait_send()
        down.wait_send()
        early.wait_send()
        far.wait_send()

    @pl.when(leaf == 1)
    def _():
        down.wait_send()
        far.wait_send()

    @pl.when(leaf == 2)
    def _():
        down.wait_send()

    exchange_wait(fbuf, 1)
    collect(fbuf, fwd_o)

    @pl.when(leaf == 0)
    def _():
        far_zero.wait_recv()

    @pl.when(leaf == 1)
    def _():
        far_one.wait_recv()

    @pl.when(leaf < 2)
    def _():
        state[1] = state[1] - product(part_in[4], matrix(1))

    @pl.when(leaf == 0)
    def _():
        side.wait_recv()
        state[1] = state[1] - part_in[5].astype(F32)

    @pl.when(leaf < 3)
    def _():
        up.wait_recv()
        part_out[4] = (state[1] - product(part_in[3], matrix(0))).astype(BF16)

    @pl.when((leaf == 1) | (leaf == 2))
    def _():
        up.start()

    @pl.when(leaf == 2)
    def _():
        part_out[5] = product(part_out[4], matrix(1)).astype(BF16)
        side.start()

    spread(part_out[4], osend, obuf, 2)
    exchange_wait(obuf, 2)
    collect(obuf, sol_o)

    @pl.when(leaf > 0)
    def _():
        up.wait_send()

    @pl.when(leaf == 2)
    def _():
        side.wait_send()

    @pl.when(leaf == 3)
    def _():
        far_one.wait_send()
        far_zero.wait_send()


def local(rhs, inverse_blocks, update_blocks, targets, widths):
    hbm = pl.BlockSpec(memory_space=pl.ANY)
    smem = pl.BlockSpec(memory_space=pltpu.SMEM)
    vmem = pl.BlockSpec(memory_space=pltpu.VMEM)
    dma = pltpu.SemaphoreType.DMA
    forward, solved = pl.pallas_call(
        kernel,
        out_shape=(jax.ShapeDtypeStruct((PIECE, W), BF16),) * 2,
        in_specs=[hbm, hbm, hbm, smem, smem],
        out_specs=(vmem, vmem),
        scratch_shapes=[
            pltpu.VMEM((PIECE, W), BF16),
            pltpu.VMEM((W, W), BF16),
            pltpu.VMEM((SLOTS, PIECE, W), BF16),
            pltpu.VMEM((2, LINE, LINE, 2, PIECE, W), BF16),
            pltpu.VMEM((GRID, PIECE, 128), BF16),
            pltpu.VMEM((GRID, PIECE, 128), BF16),
            pltpu.VMEM((GRID, PIECE, 128), BF16),
            pltpu.VMEM((128, W), F32),
            pltpu.VMEM((GRID, PIECE, 128), BF16),
            pltpu.VMEM((GRID, PIECE, 128), BF16),
            pltpu.VMEM((6, PIECE, W), BF16),
            pltpu.VMEM((6, PIECE, W), BF16),
            pltpu.VMEM((2, PIECE, W), F32),
            dma((3,)),
            dma((2, 2, 19)),
            dma((2, 2, 19)),
            dma((3,)),
            dma((3,)),
            dma((9,)),
            dma((9,)),
        ],
        compiler_params=pltpu.CompilerParams(
            collective_id=0, has_side_effects=True, vmem_limit_bytes=48 << 20
        ),
        name="solve",
    )(rhs[0], inverse_blocks[0], update_blocks[0], targets[0, :, 0], widths)
    return forward[None], solved[None]


def solution(mesh):
    placed = (
        P("leaf", "grid", None),
        P("leaf", None, None),
        P("leaf", None, "grid", None),
        P("leaf", None, "grid"),
        P("leaf"),
    )
    return jax.shard_map(
        local,
        mesh=mesh,
        in_specs=placed,
        out_specs=(P("leaf", "grid", None), P("leaf", "grid", None)),
        check_vma=False,
    )
```

```python
import jax
import jax.numpy as jnp
from jax import lax
from jax.experimental import pallas as pl
from jax.experimental.pallas import tpu as pltpu
from jax.sharding import PartitionSpec as P

MESH = pl.DeviceIdType.MESH
W = 1024
PIECE = 32
GRID = 32
LINE = 4
SLOTS = 8
HALF = W // 2
NEAR = (0, -1, 1, 2)
F32 = jnp.float32
BF16 = jnp.bfloat16


def product(a, b, transposed=False):
    dims = (((1,), (1 if transposed else 0,)), ((), ()))
    return lax.dot_general(a, b, dims, preferred_element_type=F32)


def kernel(
    rhs_h, inv_h, upd_h, tgt_h, wid_h, fwd_o, sol_o,
    rhs_v, inv_v, upd_v, tgt_s, wid_s, mats, rbuf, fbuf, obuf, wide, fsend, osend,
    part_out, part_in, state, acc,
    in_sem, gat_send, gat_recv, all_send, all_recv, hop_send, hop_recv,
):
    leaf = lax.axis_index("leaf")
    g = lax.axis_index("grid")
    z, y, c = g // 8, (g // 2) % LINE, g % 2
    place = (z, y)

    def device(x, zz, yy, cc):
        return (x, ((zz % LINE) * LINE + (yy % LINE)) * 2 + cc)

    loads = [
        pltpu.make_async_copy(upd_h, upd_v, in_sem.at[0]),
        pltpu.make_async_copy(inv_h, inv_v, in_sem.at[1]),
        pltpu.make_async_copy(rhs_h, rhs_v, in_sem.at[2]),
        pltpu.make_async_copy(tgt_h, tgt_s, in_sem.at[3]),
        pltpu.make_async_copy(wid_h, wid_s, in_sem.at[4]),
    ]
    for load in loads:
        load.start()

    barrier = pltpu.get_barrier_semaphore()

    def greet(d, carry):
        pl.semaphore_signal(barrier, inc=1, device_id=(leaf, (g + d) % GRID), device_id_type=MESH)
        return carry

    lax.fori_loop(1, GRID, greet, 0)
    for d in (1, 2, 3):
        pl.semaphore_signal(barrier, inc=1, device_id=((leaf + d) % 4, g), device_id_type=MESH)

    loads[3].wait()
    loads[4].wait()
    width = wid_s[0]

    def live(rows):
        return lax.broadcasted_iota(jnp.int32, (rows, W), 1) < width

    loads[0].wait()
    rows = []
    for t in (leaf + 1, 3, 2):
        total = jnp.zeros((PIECE, W), F32)
        for u in range(SLOTS):
            total = total + jnp.where(tgt_s[u] == t, 1.0, 0.0) * upd_v[u].astype(F32)
        rows.append(total)
    stacked = jnp.where(live(3 * PIECE), jnp.concatenate(rows, axis=0), 0.0).astype(BF16)
    loads[1].wait()
    coupling = jnp.where(live(3 * PIECE), product(stacked, inv_v[...]), 0.0).astype(BF16)

    @pl.when(leaf < 2)
    def _():
        mats[0, z, y, c] = coupling[:PIECE]

    @pl.when(leaf == 0)
    def _():
        mats[1, z, y, c] = coupling[PIECE : 2 * PIECE]
        part_out[3] = coupling[2 * PIECE :]

    @pl.when(leaf == 1)
    def _():
        part_out[3] = coupling[PIECE : 2 * PIECE]

    @pl.when(leaf == 2)
    def _():
        part_out[3] = coupling[:PIECE]

    loads[2].wait()
    pl.semaphore_wait(barrier, GRID - 1 + 3)

    def block(j, h, i1, i2):
        if h == 0:
            return mats.at[j, i1 % LINE, i2 % LINE, c, :, pl.ds(0, HALF)]
        return mats.at[j, i2 % LINE, i1 % LINE, c, :, pl.ds(HALF, HALF)]

    def bundle(j, h, i2, core):
        if h == 0:
            return mats.at[j, :, i2 % LINE, core, :, pl.ds(0, HALF)]
        return mats.at[j, i2 % LINE, :, core, :, pl.ds(HALF, HALF)]

    def there(h, i1, i2, core):
        return device(leaf, i1, i2, core) if h == 0 else device(leaf, i2, i1, core)

    def gather_copy(ref, j, h, slot, to):
        return pltpu.make_async_remote_copy(
            ref, ref, gat_send.at[j, h, slot], gat_recv.at[j, h, slot], device_id=to, device_id_type=MESH
        )

    def send(ref, j, h, slot, to):
        gather_copy(ref, j, h, slot, to).start()

    def arrived(ref, j, h, slot):
        gather_copy(ref, j, h, slot, there(0, z, y, 1 - c)).wait_recv()

    def own(h):
        return place if h == 0 else (place[1], place[0])

    def to_sibling(j, h, slot, i2):
        p1, p2 = own(h)
        send(bundle(j, h, i2, c), j, h, slot, there(h, p1, p2, 1 - c))

    def gather_first(j):
        for i, d in enumerate((1, -1, 2)):
            for h in range(2):
                p1, p2 = own(h)
                send(block(j, h, p1, p2), j, h, i, there(h, p1 + d, p2, c))

    def gather_second(j):
        for i, k in enumerate(NEAR):
            for h in range(2):
                p1, p2 = own(h)
                ref = block(j, h, p1 + k, p2)
                if k:
                    arrived(ref, j, h, i - 1)
                for e, d in enumerate((1, -1)):
                    send(ref, j, h, 3 + 2 * i + e, there(h, p1, p2 + d, c))
        for h in range(2):
            to_sibling(j, h, 15, own(h)[1])

    def gather_third(j):
        for i, k in enumerate(NEAR):
            for h in range(2):
                p1, p2 = own(h)
                for e, d in enumerate((1, -1)):
                    ref = block(j, h, p1 + k, p2 - d)
                    arrived(ref, j, h, 3 + 2 * i + e)
                    if i % 2 == e:
                        send(ref, j, h, 11 + i, there(h, p1, p2 + d, c))
        for h in range(2):
            p2 = own(h)[1]
            to_sibling(j, h, 16, p2 - 1)
            to_sibling(j, h, 17, p2 + 1)

    def gather_last(j):
        for h in range(2):
            p1, p2 = own(h)
            for i, k in enumerate(NEAR):
                arrived(block(j, h, p1 + k, p2 + 2), j, h, 11 + i)
            to_sibling(j, h, 18, p2 + 2)

    def gather_wait(j):
        for h in range(2):
            p2 = own(h)[1]
            for slot, d in ((15, 0), (16, -1), (17, 1), (18, 2)):
                arrived(bundle(j, h, p2 + d, 1 - c), j, h, slot)

    def exchange(source, target, sem):
        def one(d, carry):
            to = (g + d) % GRID
            pltpu.make_async_remote_copy(
                source(to), target.at[g], all_send.at[sem], all_recv.at[sem], device_id=(leaf, to), device_id_type=MESH
            ).start()
            return carry

        lax.fori_loop(1, GRID, one, 0)

    def exchange_wait(target, sem):
        most = target.at[pl.ds(0, GRID - 1)]
        whole = pltpu.make_async_remote_copy(
            most, most, all_send.at[sem], all_recv.at[sem], device_id=(leaf, (g + 1) % GRID), device_id_type=MESH
        )
        whole.wait_recv()
        whole.wait_send()

    def rhs_columns(to):
        return rhs_v.at[:, pl.ds(pl.multiple_of((to // 4) * 128, 128), 128)]

    def hop(source, target, slot, x):
        return pltpu.make_async_remote_copy(
            source, target, hop_send.at[slot], hop_recv.at[slot], device_id=(x, g), device_id_type=MESH
        )

    own_rows = [mats.at[j, z, y, c] for j in range(2)]
    move_near = hop(part_out.at[3], own_rows[0], 3, jnp.where(leaf == 0, 2, 3))
    move_far = hop(part_out.at[3], own_rows[1], 4, 3)
    two_jobs = (leaf == 0) | (leaf == 3)

    @pl.when(leaf == 1)
    def _():
        move_far.start()

    @pl.when((leaf == 0) | (leaf == 2))
    def _():
        move_near.start()

    @pl.when(leaf < 2)
    def _():
        gather_first(0)

    exchange(rhs_columns, rbuf, 0)
    rbuf[g] = rhs_v[:, pl.ds(pl.multiple_of((g // 4) * 128, 128), 128)]

    @pl.when(leaf >= 2)
    def _():
        move_near.wait_recv()
        gather_first(0)

    gather_second(0)

    @pl.when(leaf == 3)
    def _():
        move_far.wait_recv()

    @pl.when(two_jobs)
    def _():
        gather_first(1)

    gather_third(0)

    @pl.when(two_jobs)
    def _():
        gather_second(1)

    exchange_wait(rbuf, 0)
    wide[...] = rbuf[...].reshape(W, 128).astype(F32).T
    mine = pl.ds(pl.multiple_of((g % 4) * PIECE, PIECE), PIECE)
    state[0] = wide[mine, :]
    wide[...] = jnp.zeros_like(wide)

    gather_last(0)
    gather_wait(0)

    def matrix(j):
        return mats[j].reshape(W, W)

    LOW, HIGH = pl.ds(0, HALF), pl.ds(HALF, HALF)
    halves = (LOW, HIGH)

    def half_rows(j, n):
        return mats[j, 2 * n : 2 * n + 2].reshape(HALF, W)

    def hops(source, target, slot, x):
        return [hop(source.at[:, part], target.at[:, part], slot + n, x) for n, part in enumerate(halves)]

    down = hops(part_out.at[0], part_in.at[0], 0, leaf + 1 - 2 * (leaf // 3))
    pass_on = hops(part_out.at[2], part_in.at[0], 0, 3)
    early = hop(part_out.at[2], part_in.at[1], 2, 2)
    far = hop(part_out.at[1], part_in.at[1], 5, 3)
    skip = hop(part_out.at[2], part_in.at[2], 6, 3)

    def correct(part):
        columns = lax.broadcasted_iota(jnp.int32, (PIECE, HALF), 1) + part.start
        part_out[2, :, part] = jnp.where(columns < width, state[0, :, part], 0.0).astype(BF16)

    @pl.when(leaf == 0)
    def _():
        for part in halves:
            correct(part)
        for n, part in enumerate(halves):
            part_out[0, :, part] = product(part_out[2], half_rows(0, n), True).astype(BF16)
            down[n].start()
        early.start()

    @pl.when(leaf == 1)
    def _():
        down[0].wait_recv()
        state[0, :, LOW] = state[0, :, LOW] - part_in[0, :, LOW].astype(F32)
        correct(LOW)
        acc[...] = product(part_out[2, :, LOW], mats[0, :, :, :, :, LOW].reshape(W, HALF), True)
        down[1].wait_recv()
        state[0, :, HIGH] = state[0, :, HIGH] - part_in[0, :, HIGH].astype(F32)
        correct(HIGH)
        for n, part in enumerate(halves):
            rest = product(part_out[2, :, HIGH], mats[0, 2 * n : 2 * n + 2, :, :, :, HIGH].reshape(HALF, HALF), True)
            part_out[0, :, part] = (acc[:, part] + rest).astype(BF16)
            down[n].start()
        skip.start()

    @pl.when(two_jobs)
    def _():
        gather_third(1)
        gather_last(1)
        gather_wait(1)

    @pl.when(leaf == 0)
    def _():
        part_out[1] = product(part_out[2], matrix(1), True).astype(BF16)
        far.start()

    @pl.when(leaf == 2)
    def _():
        early.wait_recv()
        state[0] = state[0] - product(part_in[1], matrix(0), True)
        for n, part in enumerate(halves):
            down[n].wait_recv()
            state[0, :, part] = state[0, :, part] - part_in[0, :, part].astype(F32)
            correct(part)
            pass_on[n].start()

    @pl.when(leaf == 3)
    def _():
        skip.wait_recv()
        state[0] = state[0] - product(part_in[2], matrix(1), True)
        far.wait_recv()
        state[0] = state[0] - part_in[1].astype(F32)
        pass_on[0].wait_recv()
        state[0] = state[0] - product(part_in[0, :, LOW], mats[0, :, :, :, :, LOW].reshape(W, HALF), True)
        pass_on[1].wait_recv()
        state[0] = state[0] - product(part_in[0, :, HIGH], mats[0, :, :, :, :, HIGH].reshape(W, HALF), True)
        for part in halves:
            correct(part)

    forward = jnp.where(live(PIECE), product(part_out[2], inv_v[...], True), 0.0).astype(BF16)
    state[1] = jnp.where(live(PIECE), product(forward, inv_v[...]), 0.0)

    ahead = hop(state.at[1], acc, 7, 3)
    jump = hops(part_out.at[6], part_in.at[3], 8, 1)
    up = hops(part_out.at[4], part_in.at[3], 8, 0)
    last_to_first = hop(part_out.at[4], part_in.at[4], 10, 0)
    back = hop(part_out.at[6], part_in.at[4], 11, 2)
    side_one = hop(part_out.at[5], part_in.at[4], 12, 1)
    side_zero = hop(part_out.at[5], part_in.at[5], 13, 0)

    def spread(piece, staged, target, sem):
        wide[mine, :] = piece.astype(F32)
        staged[...] = wide[...].T.astype(BF16).reshape(GRID, PIECE, 128)
        exchange(lambda to: staged.at[to], target, sem)
        target[g] = staged[g]

    def collect(target, out):
        for k in range(GRID // 4):
            total = target[4 * k]
            for q in range(1, 4):
                total = total + target[4 * k + q]
            out[:, k * 128 : (k + 1) * 128] = total

    @pl.when(leaf == 2)
    def _():
        ahead.start()

    @pl.when(leaf == 3)
    def _():
        part_out[4] = state[1].astype(BF16)
        last_to_first.start()
        ahead.wait_recv()
        for n, part in enumerate(halves):
            term = product(part_out[4], mats[0, :, :, :, :, part].reshape(W, HALF))
            part_out[6, :, part] = (acc[:, part] - term).astype(BF16)
            jump[n].start()
        back.start()
        part_out[5] = product(part_out[4], matrix(1)).astype(BF16)
        side_one.start()

    spread(forward, fsend, fbuf, 1)

    @pl.when(leaf == 0)
    def _():
        last_to_first.wait_recv()
        state[1] = state[1] - product(part_in[4], matrix(1))

    @pl.when(leaf < 2)
    def _():
        up[0].wait_recv()
        acc[...] = state[1] - product(part_in[3, :, LOW], half_rows(0, 0))

    @pl.when(leaf == 1)
    def _():
        side_one.wait_recv()
        acc[...] = acc[...] - part_in[4].astype(F32)

    @pl.when(leaf == 0)
    def _():
        side_zero.wait_recv()
        acc[...] = acc[...] - part_in[5].astype(F32)

    @pl.when(leaf < 2)
    def _():
        up[1].wait_recv()
        for n, part in enumerate(halves):
            term = product(part_in[3, :, HIGH], mats[0, 2:, :, :, :, part].reshape(HALF, HALF))
            part_out[4, :, part] = (acc[:, part] - term).astype(BF16)

            @pl.when(leaf == 1)
            def _():
                up[n].start()

    @pl.when(leaf == 2)
    def _():
        back.wait_recv()
        part_out[4] = part_in[4]
        part_out[5] = product(part_in[4], matrix(0)).astype(BF16)
        side_zero.start()

    spread(part_out[4], osend, obuf, 2)

    exchange_wait(fbuf, 1)
    collect(fbuf, fwd_o)

    def gather_sent(j):
        for h in range(2):
            p1, p2 = own(h)
            for slot in range(19):
                ref = block(j, h, p1, p2) if slot < 15 else bundle(j, h, p2, c)
                gather_copy(ref, j, h, slot, there(h, p1, p2, 1 - c)).wait_send()

    gather_sent(0)

    @pl.when(two_jobs)
    def _():
        gather_sent(1)

    def sent(when, copies):
        @pl.when(when)
        def _():
            for copy in copies:
                copy.wait_send()

    sent(leaf == 0, [move_near, *down, early, far])
    sent(leaf == 1, [move_far, *down, skip, *up])
    sent(leaf == 2, [move_near, *pass_on, ahead, side_zero])
    sent(leaf == 3, [last_to_first, *jump, back, side_one])

    exchange_wait(obuf, 2)
    collect(obuf, sol_o)


def local(rhs, inverse_blocks, update_blocks, targets, widths):
    hbm = pl.BlockSpec(memory_space=pltpu.HBM)
    vmem = pl.BlockSpec(memory_space=pltpu.VMEM)
    dma = pltpu.SemaphoreType.DMA
    forward, solved = pl.pallas_call(
        kernel,
        out_shape=(jax.ShapeDtypeStruct((PIECE, W), BF16),) * 2,
        in_specs=[hbm] * 5,
        out_specs=(vmem, vmem),
        scratch_shapes=[
            pltpu.VMEM((PIECE, W), BF16),
            pltpu.VMEM((W, W), BF16),
            pltpu.VMEM((SLOTS, PIECE, W), BF16),
            pltpu.SMEM((SLOTS,), jnp.int32),
            pltpu.SMEM((1,), jnp.int32),
            pltpu.VMEM((2, LINE, LINE, 2, PIECE, W), BF16),
            pltpu.VMEM((GRID, PIECE, 128), BF16),
            pltpu.VMEM((GRID, PIECE, 128), BF16),
            pltpu.VMEM((GRID, PIECE, 128), BF16),
            pltpu.VMEM((128, W), F32),
            pltpu.VMEM((GRID, PIECE, 128), BF16),
            pltpu.VMEM((GRID, PIECE, 128), BF16),
            pltpu.VMEM((7, PIECE, W), BF16),
            pltpu.VMEM((6, PIECE, W), BF16),
            pltpu.VMEM((2, PIECE, W), F32),
            pltpu.VMEM((PIECE, W), F32),
            dma((5,)),
            dma((2, 2, 19)),
            dma((2, 2, 19)),
            dma((3,)),
            dma((3,)),
            dma((14,)),
            dma((14,)),
        ],
        compiler_params=pltpu.CompilerParams(
            collective_id=0, has_side_effects=True, vmem_limit_bytes=60 << 20
        ),
        name="solve",
    )(rhs[0], inverse_blocks[0], update_blocks[0], targets[0, :, 0], widths)
    return forward[None], solved[None]


def solution(mesh):
    placed = (
        P("leaf", "grid", None),
        P("leaf", None, None),
        P("leaf", None, "grid", None),
        P("leaf", None, "grid"),
        P("leaf"),
    )
    return jax.shard_map(
        local,
        mesh=mesh,
        in_specs=placed,
        out_specs=(P("leaf", "grid", None), P("leaf", "grid", None)),
        check_vma=False,
    )
```

```python
import jax
import jax.numpy as jnp
from jax import lax
from jax.experimental import pallas as pl
from jax.experimental.pallas import tpu as pltpu
from jax.sharding import PartitionSpec as P

MESH = pl.DeviceIdType.MESH
W = 1024
PIECE = 32
GRID = 32
LINE = 4
SLOTS = 8
HALF = W // 2
NEAR = (0, -1, 1, 2)
F32 = jnp.float32
BF16 = jnp.bfloat16


def product(a, b, transposed=False):
    dims = (((1,), (1 if transposed else 0,)), ((), ()))
    return lax.dot_general(a, b, dims, preferred_element_type=F32)


def kernel(
    rhs_h, inv_h, upd_h, tgt_h, wid_h, fwd_o, sol_o,
    rhs_v, inv_v, upd_v, tgt_s, wid_s, gram, mats, rbuf, fbuf, obuf,
    part_out, part_in, state, acc,
    in_sem, gat_send, gat_recv, all_send, all_recv, hop_send, hop_recv,
):
    leaf = lax.axis_index("leaf")
    g = lax.axis_index("grid")
    z, y, c = g // 8, (g // 2) % LINE, g % 2
    place = (z, y)

    def device(x, zz, yy, cc):
        return (x, ((zz % LINE) * LINE + (yy % LINE)) * 2 + cc)

    loads = [
        pltpu.make_async_copy(upd_h, upd_v, in_sem.at[0]),
        pltpu.make_async_copy(inv_h, inv_v, in_sem.at[1]),
        pltpu.make_async_copy(rhs_h, rhs_v, in_sem.at[2]),
        pltpu.make_async_copy(tgt_h, tgt_s, in_sem.at[3]),
        pltpu.make_async_copy(wid_h, wid_s, in_sem.at[4]),
    ]
    for load in loads:
        load.start()

    barrier = pltpu.get_barrier_semaphore()

    def greet(d, carry):
        pl.semaphore_signal(barrier, inc=1, device_id=(leaf, (g + d) % GRID), device_id_type=MESH)
        return carry

    lax.fori_loop(1, GRID, greet, 0)
    for d in (1, 2, 3):
        pl.semaphore_signal(barrier, inc=1, device_id=((leaf + d) % 4, g), device_id_type=MESH)

    loads[3].wait()
    loads[4].wait()
    width = wid_s[0]

    def live(rows):
        return lax.broadcasted_iota(jnp.int32, (rows, W), 1) < width

    loads[0].wait()

    def rows_for(t):
        total = jnp.zeros((PIECE, W), F32)
        for u in range(SLOTS):
            total = total + jnp.where(tgt_s[u] == t, 1.0, 0.0) * upd_v[u].astype(F32)
        return jnp.where(live(PIECE), total, 0.0).astype(BF16)

    def coupling(stacked):
        size = stacked.shape[0]
        return jnp.where(live(size), product(stacked, inv_v[...]), 0.0).astype(BF16)

    first = rows_for(leaf + 1)
    loads[1].wait()
    mats[jnp.where(leaf < 2, 0, 2), z, y, c] = coupling(first)
    pl.semaphore_wait(barrier, GRID - 1 + 3)

    def block(j, h, i1, i2, core=c):
        if h == 0:
            return mats.at[j, i1 % LINE, i2 % LINE, core, :, pl.ds(0, HALF)]
        return mats.at[j, i2 % LINE, i1 % LINE, core, :, pl.ds(HALF, HALF)]

    def bundle(j, h, i2, core):
        if h == 0:
            return mats.at[j, :, i2 % LINE, core, :, pl.ds(0, HALF)]
        return mats.at[j, i2 % LINE, :, core, :, pl.ds(HALF, HALF)]

    def there(h, i1, i2, core):
        return device(leaf, i1, i2, core) if h == 0 else device(leaf, i2, i1, core)

    def gather_copy(ref, j, h, slot, group, to):
        return pltpu.make_async_remote_copy(
            ref, ref, gat_send.at[j, h, group], gat_recv.at[j, h, slot], device_id=to, device_id_type=MESH
        )

    def send(ref, j, h, slot, group, to):
        gather_copy(ref, j, h, slot, group, to).start()

    def arrived(ref, j, h, slot):
        gather_copy(ref, j, h, slot, 0, there(0, z, y, 1 - c)).wait_recv()

    def own(h):
        return place if h == 0 else (place[1], place[0])

    def sibling(h):
        p1, p2 = own(h)
        return there(h, p1, p2, 1 - c)

    def gather_first(j):
        for i, d in ((2, 2), (0, 1), (1, -1)):
            for h in range(2):
                p1, p2 = own(h)
                send(block(j, h, p1, p2), j, h, i, 0, there(h, p1 + d, p2, c))

    def gather_second(j):
        for i, k in enumerate(NEAR):
            for h in range(2):
                p1, p2 = own(h)
                ref = block(j, h, p1 + k, p2)
                if k:
                    arrived(ref, j, h, i - 1)
                for e, d in enumerate((1, -1)):
                    send(ref, j, h, 3 + 2 * i + e, 1, there(h, p1, p2 + d, c))
        for h in range(2):
            send(bundle(j, h, own(h)[1], c), j, h, 15, 3, sibling(h))

    def gather_third(j):
        for i, k in enumerate(NEAR):
            for h in range(2):
                p1, p2 = own(h)
                for e, d in enumerate((1, -1)):
                    ref = block(j, h, p1 + k, p2 - d)
                    arrived(ref, j, h, 3 + 2 * i + e)
                    if i % 2 == e:
                        send(ref, j, h, 11 + i, 2, there(h, p1, p2 + d, c))
                    send(ref, j, h, 16 + 2 * i + e, 4, sibling(h))

    def gather_last(j):
        for i, k in enumerate(NEAR):
            for h in range(2):
                p1, p2 = own(h)
                ref = block(j, h, p1 + k, p2 + 2)
                arrived(ref, j, h, 11 + i)
                send(ref, j, h, 24 + i, 5, sibling(h))

    def gather_wait(j):
        for h in range(2):
            p1, p2 = own(h)
            arrived(bundle(j, h, p2, 1 - c), j, h, 15)
            for i, k in enumerate(NEAR):
                for e, d in enumerate((1, -1)):
                    arrived(block(j, h, p1 + k, p2 - d, 1 - c), j, h, 16 + 2 * i + e)
        for h in range(2):
            p1, p2 = own(h)
            for i, k in enumerate(NEAR):
                arrived(block(j, h, p1 + k, p2 + 2, 1 - c), j, h, 24 + i)

    def gather_sent(j):
        for h, part in enumerate((pl.ds(0, HALF), pl.ds(HALF, HALF))):
            for group, size in enumerate((3, 8, 4, 4, 8, 4)):
                if size == 8:
                    ref = mats.at[j, pl.ds(0, 2), :, c, :, part]
                else:
                    ref = mats.at[j, 0, pl.ds(0, size), c, :, part]
                gather_copy(ref, j, h, 0, group, sibling(h)).wait_send()

    def exchange(source, target, sem):
        for dz in (2, 1, 3, 0):
            for dy in (2, 1, 3, 0):
                for dc in (1, 0):
                    if dz or dy or dc:
                        to = (((z + dz) % LINE) * LINE + (y + dy) % LINE) * 2 + (c + dc) % 2
                        pltpu.make_async_remote_copy(
                            source(to),
                            target.at[g],
                            all_send.at[sem],
                            all_recv.at[sem],
                            device_id=(leaf, to),
                            device_id_type=MESH,
                        ).start()

    def exchange_wait(target, sem):
        most = target.at[pl.ds(0, GRID - 1)]
        whole = pltpu.make_async_remote_copy(
            most, most, all_send.at[sem], all_recv.at[sem], device_id=(leaf, (g + 1) % GRID), device_id_type=MESH
        )
        whole.wait_recv()
        whole.wait_send()

    def around(device_index):
        return pl.ds(pl.multiple_of((device_index // 4) * 128, 128), 128)

    def spread(source, target, sem):
        exchange(lambda to: source.at[:, around(to)], target, sem)
        target[g] = source[:, around(g)]

    def collect(target):
        lane = lax.broadcasted_iota(jnp.int32, (PIECE, 128), 1)
        row = lax.broadcasted_iota(jnp.int32, (PIECE, 128), 0)
        pick = jnp.where(lane == row + (g % 4) * PIECE, 1.0, 0.0).astype(BF16)
        return product(pick, target[...].reshape(W, 128), True)

    def hop(source, target, slot, x):
        return pltpu.make_async_remote_copy(
            source, target, hop_send.at[slot], hop_recv.at[slot], device_id=(x, g), device_id_type=MESH
        )

    own_rows = [mats.at[j, z, y, c] for j in range(3)]
    move_near = hop(own_rows[2], own_rows[0], 3, jnp.where(leaf == 0, 2, 3))
    move_far = hop(own_rows[2], own_rows[1], 4, 3)
    two_jobs = (leaf == 0) | (leaf == 3)

    @pl.when(leaf < 2)
    def _():
        gather_first(0)

    @pl.when(leaf == 2)
    def _():
        move_near.start()

    @pl.when(leaf < 2)
    def _():
        others = coupling(jnp.concatenate([rows_for(3), rows_for(2)], axis=0))
        near, far = others[:PIECE], others[PIECE:]
        mats[1, z, y, c] = near
        mats[2, z, y, c] = jnp.where(leaf == 0, far, near)

    @pl.when(leaf == 0)
    def _():
        move_near.start()

    @pl.when(leaf == 1)
    def _():
        move_far.start()

    loads[2].wait()
    spread(rhs_v, rbuf, 0)

    @pl.when(leaf >= 2)
    def _():
        def strip(r, carry):
            part = pl.ds(pl.multiple_of(r * 256, 256), 256)
            kept = lax.broadcasted_iota(jnp.int32, (256, W), 0) + r * 256 < width
            inv_v[part, :] = jnp.where(kept, inv_v[part, :].astype(F32), 0.0).astype(BF16)
            return carry

        lax.fori_loop(0, 4, strip, 0)

        def column(r, carry):
            part = pl.ds(pl.multiple_of(r * 256, 256), 256)
            gram[:, part] = lax.dot_general(
                inv_v[...], inv_v[:, part], (((0,), (0,)), ((), ())), preferred_element_type=F32
            ).astype(BF16)
            return carry

        lax.fori_loop(0, 4, column, 0)
        move_near.wait_recv()
        gather_first(0)

    gather_second(0)

    @pl.when(leaf == 3)
    def _():
        move_far.wait_recv()

    @pl.when(two_jobs)
    def _():
        gather_first(1)

    gather_third(0)

    @pl.when(two_jobs)
    def _():
        gather_second(1)

    exchange_wait(rbuf, 0)
    state[0] = collect(rbuf)

    gather_last(0)
    gather_wait(0)

    def matrix(j):
        return mats[j].reshape(W, W)

    LOW, HIGH = pl.ds(0, HALF), pl.ds(HALF, HALF)
    halves = (LOW, HIGH)

    def half_rows(j, n):
        return mats[j, 2 * n : 2 * n + 2].reshape(HALF, W)

    def hops(source, target, slot, x):
        return [hop(source.at[:, part], target.at[:, part], slot + n, x) for n, part in enumerate(halves)]

    down = hops(part_out.at[0], part_in.at[0], 0, leaf + 1 - 2 * (leaf // 3))
    pass_on = hops(part_out.at[2], part_in.at[0], 0, 3)
    early = hop(part_out.at[2], part_in.at[1], 2, 2)
    far = hop(part_out.at[1], part_in.at[1], 5, 3)
    skip = hop(part_out.at[2], part_in.at[2], 6, 3)

    def correct(part):
        columns = lax.broadcasted_iota(jnp.int32, (PIECE, HALF), 1) + part.start
        part_out[2, :, part] = jnp.where(columns < width, state[0, :, part], 0.0).astype(BF16)

    @pl.when(leaf == 0)
    def _():
        for part in halves:
            correct(part)
        for n, part in enumerate(halves):
            part_out[0, :, part] = product(part_out[2], half_rows(0, n), True).astype(BF16)
            down[n].start()
        early.start()

    @pl.when(leaf < 2)
    def _():
        gather_first(2)

    @pl.when(leaf == 1)
    def _():
        down[0].wait_recv()
        state[0, :, LOW] = state[0, :, LOW] - part_in[0, :, LOW].astype(F32)
        correct(LOW)
        acc[...] = product(part_out[2, :, LOW], mats[0, :, :, :, :, LOW].reshape(W, HALF), True)
        down[1].wait_recv()
        state[0, :, HIGH] = state[0, :, HIGH] - part_in[0, :, HIGH].astype(F32)
        correct(HIGH)
        for n, part in enumerate(halves):
            rest = product(part_out[2, :, HIGH], mats[0, 2 * n : 2 * n + 2, :, :, :, HIGH].reshape(HALF, HALF), True)
            part_out[0, :, part] = (acc[:, part] + rest).astype(BF16)
            down[n].start()
        skip.start()

    @pl.when(two_jobs)
    def _():
        gather_third(1)

    @pl.when(leaf < 2)
    def _():
        gather_second(2)

    @pl.when(two_jobs)
    def _():
        gather_last(1)
        gather_wait(1)

    @pl.when(leaf == 0)
    def _():
        part_out[1] = product(part_out[2], matrix(1), True).astype(BF16)
        far.start()

    @pl.when(leaf == 2)
    def _():
        early.wait_recv()
        state[0] = state[0] - product(part_in[1], matrix(0), True)
        for n, part in enumerate(halves):
            down[n].wait_recv()
            state[0, :, part] = state[0, :, part] - part_in[0, :, part].astype(F32)
            correct(part)
            pass_on[n].start()

    @pl.when(leaf == 3)
    def _():
        skip.wait_recv()
        state[0] = state[0] - product(part_in[2], matrix(1), True)
        far.wait_recv()
        state[0] = state[0] - part_in[1].astype(F32)
        pass_on[0].wait_recv()
        state[0] = state[0] - product(part_in[0, :, LOW], mats[0, :, :, :, :, LOW].reshape(W, HALF), True)
        pass_on[1].wait_recv()
        state[0] = state[0] - product(part_in[0, :, HIGH], mats[0, :, :, :, :, HIGH].reshape(W, HALF), True)
        for part in halves:
            correct(part)

    ahead = hops(part_out.at[5], part_in.at[5], 14, 3)
    jump = hops(part_out.at[6], part_in.at[3], 8, 1)
    up = hops(part_out.at[4], part_in.at[3], 8, 0)
    last_to_zero = hop(part_out.at[4], part_in.at[4], 10, 0)
    last_to_one = hop(part_out.at[4], part_in.at[4], 12, 1)
    back = hop(part_out.at[6], part_in.at[4], 11, 2)
    across = hop(part_out.at[6], part_in.at[5], 13, 0)

    @pl.when(leaf == 2)
    def _():
        for n, part in enumerate(halves):
            columns = lax.broadcasted_iota(jnp.int32, (PIECE, HALF), 1) + part.start
            own_part = jnp.where(columns < width, product(part_out[2], gram[:, part]), 0.0)
            part_out[5, :, part] = own_part.astype(BF16)
            ahead[n].start()

    @pl.when(leaf == 3)
    def _():
        part_out[4] = jnp.where(live(PIECE), product(part_out[2], gram[...]), 0.0).astype(BF16)
        last_to_one.start()
        for n, part in enumerate(halves):
            term = product(part_out[4], mats[0, :, :, :, :, part].reshape(W, HALF))
            ahead[n].wait_recv()
            part_out[6, :, part] = (part_in[5, :, part].astype(F32) - term).astype(BF16)
            jump[n].start()
        last_to_zero.start()
        across.start()
        back.start()

    forward = jnp.where(live(PIECE), product(part_out[2], inv_v[...], True), 0.0).astype(BF16)

    @pl.when(leaf < 2)
    def _():
        state[1] = jnp.where(live(PIECE), product(forward, inv_v[...]), 0.0)
        gather_third(2)

    part_out[7] = forward
    spread(part_out.at[7], fbuf, 1)

    @pl.when(leaf < 2)
    def _():
        gather_last(2)
        gather_wait(2)

    @pl.when(leaf == 0)
    def _():
        last_to_zero.wait_recv()
        state[1] = state[1] - product(part_in[4], matrix(1))
        across.wait_recv()
        state[1] = state[1] - product(part_in[5], matrix(2))

    @pl.when(leaf == 1)
    def _():
        last_to_one.wait_recv()
        state[1] = state[1] - product(part_in[4], matrix(2))

    @pl.when(leaf < 2)
    def _():
        up[0].wait_recv()
        acc[...] = state[1] - product(part_in[3, :, LOW], half_rows(0, 0))
        up[1].wait_recv()
        for n, part in enumerate(halves):
            term = product(part_in[3, :, HIGH], mats[0, 2:, :, :, :, part].reshape(HALF, HALF))
            part_out[4, :, part] = (acc[:, part] - term).astype(BF16)

            @pl.when(leaf == 1)
            def _():
                up[n].start()

    @pl.when(leaf == 2)
    def _():
        back.wait_recv()
        part_out[4] = part_in[4]

    spread(part_out.at[4], obuf, 2)

    exchange_wait(fbuf, 1)
    fwd_o[...] = collect(fbuf).astype(BF16)

    gather_sent(0)

    @pl.when(two_jobs)
    def _():
        gather_sent(1)

    @pl.when(leaf < 2)
    def _():
        gather_sent(2)

    def sent(when, copies):
        @pl.when(when)
        def _():
            for copy in copies:
                copy.wait_send()

    sent(leaf == 0, [move_near, *down, early, far])
    sent(leaf == 1, [move_far, *down, skip, *up])
    sent(leaf == 2, [move_near, *pass_on, *ahead])
    sent(leaf == 3, [last_to_one, *jump, last_to_zero, across, back])

    exchange_wait(obuf, 2)
    sol_o[...] = collect(obuf).astype(BF16)


def local(rhs, inverse_blocks, update_blocks, targets, widths):
    hbm = pl.BlockSpec(memory_space=pltpu.HBM)
    vmem = pl.BlockSpec(memory_space=pltpu.VMEM)
    dma = pltpu.SemaphoreType.DMA
    forward, solved = pl.pallas_call(
        kernel,
        out_shape=(jax.ShapeDtypeStruct((PIECE, W), BF16),) * 2,
        in_specs=[hbm] * 5,
        out_specs=(vmem, vmem),
        scratch_shapes=[
            pltpu.VMEM((PIECE, W), BF16),
            pltpu.VMEM((W, W), BF16),
            pltpu.VMEM((SLOTS, PIECE, W), BF16),
            pltpu.SMEM((SLOTS,), jnp.int32),
            pltpu.SMEM((1,), jnp.int32),
            pltpu.VMEM((W, W), BF16),
            pltpu.VMEM((3, LINE, LINE, 2, PIECE, W), BF16),
            pltpu.VMEM((GRID, PIECE, 128), BF16),
            pltpu.VMEM((GRID, PIECE, 128), BF16),
            pltpu.VMEM((GRID, PIECE, 128), BF16),
            pltpu.VMEM((8, PIECE, W), BF16),
            pltpu.VMEM((6, PIECE, W), BF16),
            pltpu.VMEM((2, PIECE, W), F32),
            pltpu.VMEM((PIECE, W), F32),
            dma((5,)),
            dma((3, 2, 6)),
            dma((3, 2, 28)),
            dma((3,)),
            dma((3,)),
            dma((16,)),
            dma((16,)),
        ],
        compiler_params=pltpu.CompilerParams(
            collective_id=0, has_side_effects=True, vmem_limit_bytes=55040 << 10
        ),
        name="solve",
    )(rhs[0], inverse_blocks[0], update_blocks[0], targets[0, :, 0], widths)
    return forward[None], solved[None]


def solution(mesh):
    placed = (
        P("leaf", "grid", None),
        P("leaf", None, None),
        P("leaf", None, "grid", None),
        P("leaf", None, "grid"),
        P("leaf"),
    )
    return jax.shard_map(
        local,
        mesh=mesh,
        in_specs=placed,
        out_specs=(P("leaf", "grid", None), P("leaf", "grid", None)),
        check_vma=False,
    )
```

```python
import jax
import jax.numpy as jnp
from jax import lax
from jax.experimental import pallas as pl
from jax.experimental.pallas import tpu as pltpu
from jax.sharding import PartitionSpec as P

MESH = pl.DeviceIdType.MESH
W = 1024
PIECE = 32
GRID = 32
LINE = 4
SLOTS = 8
HALF = W // 2
NEAR = (0, -1, 1, 2)
OTHERS = [(dz, dy, dc) for dz in (2, 1, 3, 0) for dy in (2, 1, 3, 0) for dc in (1, 0) if dz or dy or dc]
F32 = jnp.float32
BF16 = jnp.bfloat16


def product(a, b, transposed=False):
    dims = (((1,), (1 if transposed else 0,)), ((), ()))
    return lax.dot_general(a, b, dims, preferred_element_type=F32)


def kernel(
    rhs_h, inv_h, upd_h, tgt_h, wid_h, fwd_o, sol_o,
    rhs_v, inv_v, upd_v, tgt_s, wid_s, gram, mats, rbuf, fbuf, obuf, packs,
    part_out, part_in, state, acc,
    in_sem, gat_send, gat_recv, all_send, all_recv, hop_send, hop_recv,
):
    leaf = lax.axis_index("leaf")
    g = lax.axis_index("grid")
    z, y, c = g // 8, (g // 2) % LINE, g % 2
    place = (z, y)

    def device(x, zz, yy, cc):
        return (x, ((zz % LINE) * LINE + (yy % LINE)) * 2 + cc)

    loads = [
        pltpu.make_async_copy(upd_h, upd_v, in_sem.at[0]),
        pltpu.make_async_copy(inv_h, inv_v, in_sem.at[1]),
        pltpu.make_async_copy(rhs_h, rhs_v, in_sem.at[2]),
        pltpu.make_async_copy(tgt_h, tgt_s, in_sem.at[3]),
        pltpu.make_async_copy(wid_h, wid_s, in_sem.at[4]),
    ]
    for load in loads:
        load.start()

    barrier = pltpu.get_barrier_semaphore()

    for d in (2, 1, 3):
        pl.semaphore_signal(barrier, inc=1, device_id=((leaf + d) % 4, g), device_id_type=MESH)
    for dz, dy, dc in OTHERS:
        to = device(leaf, z + dz, y + dy, (c + dc) % 2)
        pl.semaphore_signal(barrier, inc=1, device_id=to, device_id_type=MESH)

    loads[3].wait()
    loads[4].wait()
    width = wid_s[0]

    def live(rows):
        return lax.broadcasted_iota(jnp.int32, (rows, W), 1) < width

    loads[0].wait()

    def rows_for(t):
        total = jnp.zeros((PIECE, W), F32)
        for u in range(SLOTS):
            total = total + jnp.where(tgt_s[u] == t, 1.0, 0.0) * upd_v[u].astype(F32)
        return jnp.where(live(PIECE), total, 0.0).astype(BF16)

    def coupling(stacked):
        size = stacked.shape[0]
        return jnp.where(live(size), product(stacked, inv_v[...]), 0.0).astype(BF16)

    first = rows_for(leaf + 1)
    loads[1].wait()
    mats[jnp.where(leaf < 2, 0, 2), z, y, c] = coupling(first)
    pl.semaphore_wait(barrier, GRID - 1 + 3)

    def block(j, h, i1, i2, core=c):
        if h == 0:
            return mats.at[j, i1 % LINE, i2 % LINE, core, :, pl.ds(0, HALF)]
        return mats.at[j, i2 % LINE, i1 % LINE, core, :, pl.ds(HALF, HALF)]

    def bundle(j, h, i2, core):
        if h == 0:
            return mats.at[j, :, i2 % LINE, core, :, pl.ds(0, HALF)]
        return mats.at[j, i2 % LINE, :, core, :, pl.ds(HALF, HALF)]

    def there(h, i1, i2, core):
        return device(leaf, i1, i2, core) if h == 0 else device(leaf, i2, i1, core)

    def gather_copy(ref, j, h, slot, group, to):
        return pltpu.make_async_remote_copy(
            ref, ref, gat_send.at[j, h, group], gat_recv.at[j, h, slot], device_id=to, device_id_type=MESH
        )

    def send(ref, j, h, slot, group, to):
        gather_copy(ref, j, h, slot, group, to).start()

    def arrived(ref, j, h, slot):
        gather_copy(ref, j, h, slot, 0, there(0, z, y, 1 - c)).wait_recv()

    def own(h):
        return place if h == 0 else (place[1], place[0])

    def sibling(h):
        p1, p2 = own(h)
        return there(h, p1, p2, 1 - c)

    def gather_first(j):
        for i, d in ((2, 2), (0, 1), (1, -1)):
            for h in range(2):
                p1, p2 = own(h)
                send(block(j, h, p1, p2), j, h, i, 0, there(h, p1 + d, p2, c))

    def gather_second(j):
        for i, k in enumerate(NEAR):
            for h in range(2):
                p1, p2 = own(h)
                ref = block(j, h, p1 + k, p2)
                if k:
                    arrived(ref, j, h, i - 1)
                for e, d in enumerate((1, -1)):
                    send(ref, j, h, 3 + 2 * i + e, 1, there(h, p1, p2 + d, c))
        for h in range(2):
            send(bundle(j, h, own(h)[1], c), j, h, 15, 3, sibling(h))

    def gather_third(j):
        for i, k in enumerate(NEAR):
            for h in range(2):
                p1, p2 = own(h)
                for e, d in enumerate((1, -1)):
                    ref = block(j, h, p1 + k, p2 - d)
                    arrived(ref, j, h, 3 + 2 * i + e)
                    if i % 2 == e:
                        send(ref, j, h, 11 + i, 2, there(h, p1, p2 + d, c))
                    send(ref, j, h, 16 + 2 * i + e, 4, sibling(h))

    def gather_last(j):
        for i, k in enumerate(NEAR):
            for h in range(2):
                p1, p2 = own(h)
                ref = block(j, h, p1 + k, p2 + 2)
                arrived(ref, j, h, 11 + i)
                send(ref, j, h, 24 + i, 5, sibling(h))

    def gather_wait(j):
        for h in range(2):
            p1, p2 = own(h)
            arrived(bundle(j, h, p2, 1 - c), j, h, 15)
            for i, k in enumerate(NEAR):
                for e, d in enumerate((1, -1)):
                    arrived(block(j, h, p1 + k, p2 - d, 1 - c), j, h, 16 + 2 * i + e)
        for h in range(2):
            p1, p2 = own(h)
            for i, k in enumerate(NEAR):
                arrived(block(j, h, p1 + k, p2 + 2, 1 - c), j, h, 24 + i)

    def gather_sent(j):
        for h, part in enumerate((pl.ds(0, HALF), pl.ds(HALF, HALF))):
            for group, size in enumerate((3, 8, 4, 4, 8, 4)):
                if size == 8:
                    ref = mats.at[j, pl.ds(0, 2), :, c, :, part]
                else:
                    ref = mats.at[j, 0, pl.ds(0, size), c, :, part]
                gather_copy(ref, j, h, 0, group, sibling(h)).wait_send()

    def exchange(source, target, sem):
        for dz, dy, dc in OTHERS:
            to = device(leaf, z + dz, y + dy, (c + dc) % 2)
            pltpu.make_async_remote_copy(
                source(to[1]),
                target.at[g],
                all_send.at[sem],
                all_recv.at[sem],
                device_id=to,
                device_id_type=MESH,
            ).start()

    def exchange_wait(target, sem):
        most = target.at[pl.ds(0, GRID - 1)]
        whole = pltpu.make_async_remote_copy(
            most, most, all_send.at[sem], all_recv.at[sem], device_id=(leaf, (g + 1) % GRID), device_id_type=MESH
        )
        whole.wait_recv()
        whole.wait_send()

    def around(device_index):
        return pl.ds(pl.multiple_of((device_index // 4) * 128, 128), 128)

    def spread(values, packed, target, sem):
        left = lax.broadcasted_iota(jnp.int32, (16, 128), 1) < 64
        for k in range(GRID // 4):
            tile = values[:, k * 128 : (k + 1) * 128].astype(F32)
            top, bottom = tile[:16], tile[16:]
            part = pl.ds(k * 128, 128)
            packed[0, :, part] = jnp.where(left, top, pltpu.roll(bottom, 64, 1)).astype(BF16)
            packed[1, :, part] = jnp.where(left, pltpu.roll(top, 64, 1), bottom).astype(BF16)
        exchange(lambda to: packed.at[(to % 4) // 2, :, around(to)], target, sem)
        target[g] = packed[(g % 4) // 2, :, around(g)]

    def collect(target):
        lane = lax.broadcasted_iota(jnp.int32, (PIECE, 128), 1)
        row = lax.broadcasted_iota(jnp.int32, (PIECE, 128), 0)
        pick = jnp.where(lane == row + (g % 2) * PIECE, 1.0, 0.0).astype(BF16)
        held = target[...].astype(F32)
        turned = pltpu.roll(held.reshape(GRID * 16, 128), 64, 1).reshape(GRID, 16, 128)
        whole = jnp.concatenate([held, turned], axis=1).reshape(W, 128).astype(BF16)
        return product(pick, whole, True)

    def hop(source, target, slot, x):
        return pltpu.make_async_remote_copy(
            source, target, hop_send.at[slot], hop_recv.at[slot], device_id=(x, g), device_id_type=MESH
        )

    own_rows = [mats.at[j, z, y, c] for j in range(3)]
    move_near = hop(own_rows[2], own_rows[0], 3, jnp.where(leaf == 0, 2, 3))
    move_far = hop(own_rows[2], own_rows[1], 4, 3)
    two_jobs = (leaf == 0) | (leaf == 3)

    @pl.when(leaf < 2)
    def _():
        gather_first(0)

    @pl.when(leaf == 2)
    def _():
        move_near.start()

    @pl.when(leaf < 2)
    def _():
        others = coupling(jnp.concatenate([rows_for(3), rows_for(2)], axis=0))
        near, far = others[:PIECE], others[PIECE:]
        mats[1, z, y, c] = near
        mats[2, z, y, c] = jnp.where(leaf == 0, far, near)

    @pl.when(leaf == 0)
    def _():
        move_near.start()

    @pl.when(leaf == 1)
    def _():
        move_far.start()

    loads[2].wait()
    spread(rhs_v[...], packs.at[0], rbuf, 0)

    @pl.when(leaf >= 2)
    def _():
        def strip(r, carry):
            part = pl.ds(pl.multiple_of(r * 256, 256), 256)
            kept = lax.broadcasted_iota(jnp.int32, (256, W), 0) + r * 256 < width
            inv_v[part, :] = jnp.where(kept, inv_v[part, :].astype(F32), 0.0).astype(BF16)
            return carry

        lax.fori_loop(0, 4, strip, 0)

        def column(r, carry):
            part = pl.ds(pl.multiple_of(r * 256, 256), 256)
            gram[:, part] = lax.dot_general(
                inv_v[...], inv_v[:, part], (((0,), (0,)), ((), ())), preferred_element_type=F32
            ).astype(BF16)
            return carry

        lax.fori_loop(0, 4, column, 0)
        move_near.wait_recv()
        gather_first(0)

    gather_second(0)

    @pl.when(leaf == 3)
    def _():
        move_far.wait_recv()

    @pl.when(two_jobs)
    def _():
        gather_first(1)

    gather_third(0)

    @pl.when(two_jobs)
    def _():
        gather_second(1)

    exchange_wait(rbuf, 0)
    state[0] = collect(rbuf)

    gather_last(0)
    gather_wait(0)

    def matrix(j):
        return mats[j].reshape(W, W)

    LOW, HIGH = pl.ds(0, HALF), pl.ds(HALF, HALF)
    halves = (LOW, HIGH)

    def half_rows(j, n):
        return mats[j, 2 * n : 2 * n + 2].reshape(HALF, W)

    def hops(source, target, slot, x):
        return [hop(source.at[:, part], target.at[:, part], slot + n, x) for n, part in enumerate(halves)]

    down = hops(part_out.at[0], part_in.at[0], 0, leaf + 1 - 2 * (leaf // 3))
    pass_on = hops(part_out.at[2], part_in.at[0], 0, 3)
    early = hop(part_out.at[2], part_in.at[1], 2, 2)
    far = hop(part_out.at[1], part_in.at[1], 5, 3)
    skip = hop(part_out.at[2], part_in.at[2], 6, 3)

    def correct(part):
        columns = lax.broadcasted_iota(jnp.int32, (PIECE, HALF), 1) + part.start
        part_out[2, :, part] = jnp.where(columns < width, state[0, :, part], 0.0).astype(BF16)

    @pl.when(leaf == 0)
    def _():
        for part in halves:
            correct(part)
        for n, part in enumerate(halves):
            part_out[0, :, part] = product(part_out[2], half_rows(0, n), True).astype(BF16)
            down[n].start()
        early.start()

    @pl.when(leaf < 2)
    def _():
        gather_first(2)

    @pl.when(leaf == 1)
    def _():
        down[0].wait_recv()
        state[0, :, LOW] = state[0, :, LOW] - part_in[0, :, LOW].astype(F32)
        correct(LOW)
        acc[...] = product(part_out[2, :, LOW], mats[0, :, :, :, :, LOW].reshape(W, HALF), True)
        down[1].wait_recv()
        state[0, :, HIGH] = state[0, :, HIGH] - part_in[0, :, HIGH].astype(F32)
        correct(HIGH)
        for n, part in enumerate(halves):
            rest = product(part_out[2, :, HIGH], mats[0, 2 * n : 2 * n + 2, :, :, :, HIGH].reshape(HALF, HALF), True)
            part_out[0, :, part] = (acc[:, part] + rest).astype(BF16)
            down[n].start()
        skip.start()

    @pl.when(two_jobs)
    def _():
        gather_third(1)

    @pl.when(leaf < 2)
    def _():
        gather_second(2)

    @pl.when(two_jobs)
    def _():
        gather_last(1)
        gather_wait(1)

    @pl.when(leaf == 0)
    def _():
        part_out[1] = product(part_out[2], matrix(1), True).astype(BF16)
        far.start()

    @pl.when(leaf == 2)
    def _():
        early.wait_recv()
        state[0] = state[0] - product(part_in[1], matrix(0), True)
        for n, part in enumerate(halves):
            down[n].wait_recv()
            state[0, :, part] = state[0, :, part] - part_in[0, :, part].astype(F32)
            correct(part)
            pass_on[n].start()

    @pl.when(leaf == 3)
    def _():
        skip.wait_recv()
        state[0] = state[0] - product(part_in[2], matrix(1), True)
        far.wait_recv()
        state[0] = state[0] - part_in[1].astype(F32)
        pass_on[0].wait_recv()
        state[0] = state[0] - product(part_in[0, :, LOW], mats[0, :, :, :, :, LOW].reshape(W, HALF), True)
        pass_on[1].wait_recv()
        state[0] = state[0] - product(part_in[0, :, HIGH], mats[0, :, :, :, :, HIGH].reshape(W, HALF), True)
        for part in halves:
            correct(part)

    ahead = hops(part_out.at[5], part_in.at[5], 14, 3)
    jump = hops(part_out.at[6], part_in.at[3], 8, 1)
    up = hops(part_out.at[4], part_in.at[3], 8, 0)
    last_to_zero = hop(part_out.at[4], part_in.at[4], 10, 0)
    last_to_one = hop(part_out.at[4], part_in.at[4], 12, 1)
    back = hop(part_out.at[6], part_in.at[4], 11, 2)
    across = hop(part_out.at[6], part_in.at[5], 13, 0)

    @pl.when(leaf == 2)
    def _():
        for n, part in enumerate(halves):
            columns = lax.broadcasted_iota(jnp.int32, (PIECE, HALF), 1) + part.start
            own_part = jnp.where(columns < width, product(part_out[2], gram[:, part]), 0.0)
            part_out[5, :, part] = own_part.astype(BF16)
            ahead[n].start()

    @pl.when(leaf == 3)
    def _():
        part_out[4] = jnp.where(live(PIECE), product(part_out[2], gram[...]), 0.0).astype(BF16)
        last_to_one.start()
        for n, part in enumerate(halves):
            term = product(part_out[4], mats[0, :, :, :, :, part].reshape(W, HALF))
            ahead[n].wait_recv()
            part_out[6, :, part] = (part_in[5, :, part].astype(F32) - term).astype(BF16)
            jump[n].start()
        last_to_zero.start()
        across.start()
        back.start()

    forward = jnp.where(live(PIECE), product(part_out[2], inv_v[...], True), 0.0).astype(BF16)

    @pl.when(leaf < 2)
    def _():
        state[1] = jnp.where(live(PIECE), product(forward, inv_v[...]), 0.0)
        gather_third(2)

    spread(forward, packs.at[1], fbuf, 1)

    @pl.when(leaf < 2)
    def _():
        gather_last(2)
        gather_wait(2)

    @pl.when(leaf == 0)
    def _():
        last_to_zero.wait_recv()
        state[1] = state[1] - product(part_in[4], matrix(1))
        across.wait_recv()
        state[1] = state[1] - product(part_in[5], matrix(2))

    @pl.when(leaf == 1)
    def _():
        last_to_one.wait_recv()
        state[1] = state[1] - product(part_in[4], matrix(2))

    @pl.when(leaf < 2)
    def _():
        up[0].wait_recv()
        acc[...] = state[1] - product(part_in[3, :, LOW], half_rows(0, 0))
        up[1].wait_recv()
        for n, part in enumerate(halves):
            term = product(part_in[3, :, HIGH], mats[0, 2:, :, :, :, part].reshape(HALF, HALF))
            part_out[4, :, part] = (acc[:, part] - term).astype(BF16)

            @pl.when(leaf == 1)
            def _():
                up[n].start()

    @pl.when(leaf == 2)
    def _():
        back.wait_recv()
        part_out[4] = part_in[4]

    spread(part_out[4], packs.at[2], obuf, 2)

    exchange_wait(fbuf, 1)
    fwd_o[...] = collect(fbuf).astype(BF16)

    gather_sent(0)

    @pl.when(two_jobs)
    def _():
        gather_sent(1)

    @pl.when(leaf < 2)
    def _():
        gather_sent(2)

    def sent(when, copies):
        @pl.when(when)
        def _():
            for copy in copies:
                copy.wait_send()

    sent(leaf == 0, [move_near, *down, early, far])
    sent(leaf == 1, [move_far, *down, skip, *up])
    sent(leaf == 2, [move_near, *pass_on, *ahead])
    sent(leaf == 3, [last_to_one, *jump, last_to_zero, across, back])

    exchange_wait(obuf, 2)
    sol_o[...] = collect(obuf).astype(BF16)


def local(rhs, inverse_blocks, update_blocks, targets, widths):
    hbm = pl.BlockSpec(memory_space=pltpu.HBM)
    vmem = pl.BlockSpec(memory_space=pltpu.VMEM)
    dma = pltpu.SemaphoreType.DMA
    forward, solved = pl.pallas_call(
        kernel,
        out_shape=(jax.ShapeDtypeStruct((PIECE, W), BF16),) * 2,
        in_specs=[hbm] * 5,
        out_specs=(vmem, vmem),
        scratch_shapes=[
            pltpu.VMEM((PIECE, W), BF16),
            pltpu.VMEM((W, W), BF16),
            pltpu.VMEM((SLOTS, PIECE, W), BF16),
            pltpu.SMEM((SLOTS,), jnp.int32),
            pltpu.SMEM((1,), jnp.int32),
            pltpu.VMEM((W, W), BF16),
            pltpu.VMEM((3, LINE, LINE, 2, PIECE, W), BF16),
            pltpu.VMEM((GRID, 16, 128), BF16),
            pltpu.VMEM((GRID, 16, 128), BF16),
            pltpu.VMEM((GRID, 16, 128), BF16),
            pltpu.VMEM((3, 2, 16, W), BF16),
            pltpu.VMEM((7, PIECE, W), BF16),
            pltpu.VMEM((6, PIECE, W), BF16),
            pltpu.VMEM((2, PIECE, W), F32),
            pltpu.VMEM((PIECE, W), F32),
            dma((5,)),
            dma((3, 2, 6)),
            dma((3, 2, 28)),
            dma((3,)),
            dma((3,)),
            dma((16,)),
            dma((16,)),
        ],
        compiler_params=pltpu.CompilerParams(
            collective_id=0, has_side_effects=True, vmem_limit_bytes=55040 << 10
        ),
        name="solve",
    )(rhs[0], inverse_blocks[0], update_blocks[0], targets[0, :, 0], widths)
    return forward[None], solved[None]


def solution(mesh):
    placed = (
        P("leaf", "grid", None),
        P("leaf", None, None),
        P("leaf", None, "grid", None),
        P("leaf", None, "grid"),
        P("leaf"),
    )
    return jax.shard_map(
        local,
        mesh=mesh,
        in_specs=placed,
        out_specs=(P("leaf", "grid", None), P("leaf", "grid", None)),
        check_vma=False,
    )
```

```python
import jax
import jax.numpy as jnp
from jax import lax
from jax.experimental import pallas as pl
from jax.experimental.pallas import tpu as pltpu
from jax.sharding import PartitionSpec as P

MESH = pl.DeviceIdType.MESH
W = 1024
PIECE = 32
GRID = 32
LINE = 4
SLOTS = 8
HALF = W // 2
NEAR = (0, -1, 1, 2)
OTHERS = [(dz, dy, dc) for dz in (2, 1, 3, 0) for dy in (2, 1, 3, 0) for dc in (1, 0) if dz or dy or dc]
F32 = jnp.float32
BF16 = jnp.bfloat16


def product(a, b, transposed=False):
    dims = (((1,), (1 if transposed else 0,)), ((), ()))
    return lax.dot_general(a, b, dims, preferred_element_type=F32)


def kernel(
    rhs_h, inv_h, upd_h, tgt_h, wid_h, fwd_o, sol_o,
    rhs_v, inv_v, upd_v, tgt_s, wid_s, gram, mats, rbuf, fbuf, obuf, packs,
    part_out, part_in, state, acc,
    in_sem, gat_send, gat_recv, all_send, all_recv, hop_send, hop_recv,
):
    leaf = lax.axis_index("leaf")
    g = lax.axis_index("grid")
    z, y, c = g // 8, (g // 2) % LINE, g % 2
    place = (z, y)

    def device(x, zz, yy, cc):
        return (x, ((zz % LINE) * LINE + (yy % LINE)) * 2 + cc)

    loads = [
        pltpu.make_async_copy(upd_h, upd_v, in_sem.at[0]),
        pltpu.make_async_copy(inv_h.at[pl.ds(0, 256)], inv_v.at[pl.ds(0, 256)], in_sem.at[1]),
        pltpu.make_async_copy(rhs_h, rhs_v, in_sem.at[2]),
        pltpu.make_async_copy(tgt_h, tgt_s, in_sem.at[3]),
        pltpu.make_async_copy(wid_h, wid_s, in_sem.at[4]),
    ]
    rest = [
        pltpu.make_async_copy(inv_h.at[pl.ds(256 * r, 256)], inv_v.at[pl.ds(256 * r, 256)], in_sem.at[4 + r])
        for r in (1, 2, 3)
    ]
    for load in (*loads[:2], *rest, *loads[2:]):
        load.start()

    barrier = pltpu.get_barrier_semaphore()

    for d in (2, 1, 3):
        pl.semaphore_signal(barrier, inc=1, device_id=((leaf + d) % 4, g), device_id_type=MESH)
    for dz, dy, dc in OTHERS:
        to = device(leaf, z + dz, y + dy, (c + dc) % 2)
        pl.semaphore_signal(barrier, inc=1, device_id=to, device_id_type=MESH)

    loads[3].wait()
    loads[4].wait()
    width = wid_s[0]

    def live(rows):
        return lax.broadcasted_iota(jnp.int32, (rows, W), 1) < width

    loads[0].wait()

    def rows_for(t):
        total = jnp.zeros((PIECE, W), F32)
        for u in range(SLOTS):
            total = total + jnp.where(tgt_s[u] == t, 1.0, 0.0) * upd_v[u].astype(F32)
        return jnp.where(live(PIECE), total, 0.0).astype(BF16)

    def coupling(stacked):
        size = stacked.shape[0]
        return jnp.where(live(size), product(stacked, inv_v[...]), 0.0).astype(BF16)

    first = rows_for(leaf + 1)
    total = jnp.zeros((PIECE, W), F32)
    for r, load in enumerate((loads[1], *rest)):
        load.wait()
        total = total + product(first[:, 256 * r : 256 * (r + 1)], inv_v[256 * r : 256 * (r + 1), :])
    mats[jnp.where(leaf < 2, 0, 2), z, y, c] = jnp.where(live(PIECE), total, 0.0).astype(BF16)
    pl.semaphore_wait(barrier, GRID - 1 + 3)

    def block(j, h, i1, i2, core=c):
        if h == 0:
            return mats.at[j, i1 % LINE, i2 % LINE, core, :, pl.ds(0, HALF)]
        return mats.at[j, i2 % LINE, i1 % LINE, core, :, pl.ds(HALF, HALF)]

    def bundle(j, h, i2, core):
        if h == 0:
            return mats.at[j, :, i2 % LINE, core, :, pl.ds(0, HALF)]
        return mats.at[j, i2 % LINE, :, core, :, pl.ds(HALF, HALF)]

    def there(h, i1, i2, core):
        return device(leaf, i1, i2, core) if h == 0 else device(leaf, i2, i1, core)

    def gather_copy(ref, j, h, slot, group, to):
        return pltpu.make_async_remote_copy(
            ref, ref, gat_send.at[j, h, group], gat_recv.at[j, h, slot], device_id=to, device_id_type=MESH
        )

    def send(ref, j, h, slot, group, to):
        gather_copy(ref, j, h, slot, group, to).start()

    def arrived(ref, j, h, slot):
        gather_copy(ref, j, h, slot, 0, there(0, z, y, 1 - c)).wait_recv()

    def own(h):
        return place if h == 0 else (place[1], place[0])

    def sibling(h):
        p1, p2 = own(h)
        return there(h, p1, p2, 1 - c)

    def gather_first(j):
        for i, d in ((2, 2), (0, 1), (1, -1)):
            for h in range(2):
                p1, p2 = own(h)
                send(block(j, h, p1, p2), j, h, i, 0, there(h, p1 + d, p2, c))

    def gather_second(j):
        for i, k in enumerate(NEAR):
            for h in range(2):
                p1, p2 = own(h)
                ref = block(j, h, p1 + k, p2)
                if k:
                    arrived(ref, j, h, i - 1)
                for e, d in enumerate((1, -1)):
                    send(ref, j, h, 3 + 2 * i + e, 1, there(h, p1, p2 + d, c))
        for h in range(2):
            send(bundle(j, h, own(h)[1], c), j, h, 15, 3, sibling(h))

    def gather_third(j):
        for i, k in enumerate(NEAR):
            for h in range(2):
                p1, p2 = own(h)
                for e, d in enumerate((1, -1)):
                    ref = block(j, h, p1 + k, p2 - d)
                    arrived(ref, j, h, 3 + 2 * i + e)
                    if i % 2 == e:
                        send(ref, j, h, 11 + i, 2, there(h, p1, p2 + d, c))
                    send(ref, j, h, 16 + 2 * i + e, 4, sibling(h))

    def gather_last(j):
        for i, k in enumerate(NEAR):
            for h in range(2):
                p1, p2 = own(h)
                ref = block(j, h, p1 + k, p2 + 2)
                arrived(ref, j, h, 11 + i)
                send(ref, j, h, 24 + i, 5, sibling(h))

    def gather_wait(j):
        for h in range(2):
            p1, p2 = own(h)
            arrived(bundle(j, h, p2, 1 - c), j, h, 15)
            for i, k in enumerate(NEAR):
                for e, d in enumerate((1, -1)):
                    arrived(block(j, h, p1 + k, p2 - d, 1 - c), j, h, 16 + 2 * i + e)
        for h in range(2):
            p1, p2 = own(h)
            for i, k in enumerate(NEAR):
                arrived(block(j, h, p1 + k, p2 + 2, 1 - c), j, h, 24 + i)

    def gather_sent(j):
        for h, part in enumerate((pl.ds(0, HALF), pl.ds(HALF, HALF))):
            for group, size in enumerate((3, 8, 4, 4, 8, 4)):
                if size == 8:
                    ref = mats.at[j, pl.ds(0, 2), :, c, :, part]
                else:
                    ref = mats.at[j, 0, pl.ds(0, size), c, :, part]
                gather_copy(ref, j, h, 0, group, sibling(h)).wait_send()

    def exchange(source, target, sem):
        for dz, dy, dc in OTHERS:
            to = device(leaf, z + dz, y + dy, (c + dc) % 2)
            pltpu.make_async_remote_copy(
                source(to[1]),
                target.at[g],
                all_send.at[sem],
                all_recv.at[sem],
                device_id=to,
                device_id_type=MESH,
            ).start()

    def exchange_wait(target, sem):
        most = target.at[pl.ds(0, GRID - 1)]
        whole = pltpu.make_async_remote_copy(
            most, most, all_send.at[sem], all_recv.at[sem], device_id=(leaf, (g + 1) % GRID), device_id_type=MESH
        )
        whole.wait_recv()
        whole.wait_send()

    def around(device_index):
        return pl.ds(pl.multiple_of((device_index // 4) * 128, 128), 128)

    def spread(values, packed, target, sem):
        left = lax.broadcasted_iota(jnp.int32, (16, 128), 1) < 64
        for k in range(GRID // 4):
            tile = values[:, k * 128 : (k + 1) * 128].astype(F32)
            top, bottom = tile[:16], tile[16:]
            part = pl.ds(k * 128, 128)
            packed[0, :, part] = jnp.where(left, top, pltpu.roll(bottom, 64, 1)).astype(BF16)
            packed[1, :, part] = jnp.where(left, pltpu.roll(top, 64, 1), bottom).astype(BF16)
        exchange(lambda to: packed.at[(to % 4) // 2, :, around(to)], target, sem)
        target[g] = packed[(g % 4) // 2, :, around(g)]

    def collect(target):
        lane = lax.broadcasted_iota(jnp.int32, (PIECE, 128), 1)
        row = lax.broadcasted_iota(jnp.int32, (PIECE, 128), 0)
        pick = jnp.where(lane == row + (g % 2) * PIECE, 1.0, 0.0).astype(BF16)
        held = target[...].astype(F32)
        turned = pltpu.roll(held.reshape(GRID * 16, 128), 64, 1).reshape(GRID, 16, 128)
        whole = jnp.concatenate([held, turned], axis=1).reshape(W, 128).astype(BF16)
        return product(pick, whole, True)

    def hop(source, target, slot, x):
        return pltpu.make_async_remote_copy(
            source, target, hop_send.at[slot], hop_recv.at[slot], device_id=(x, g), device_id_type=MESH
        )

    own_rows = [mats.at[j, z, y, c] for j in range(3)]
    move_near = hop(own_rows[2], own_rows[0], 3, jnp.where(leaf == 0, 2, 3))
    move_far = hop(own_rows[2], own_rows[1], 4, 3)
    two_jobs = (leaf == 0) | (leaf == 3)

    @pl.when(leaf < 2)
    def _():
        gather_first(0)

    @pl.when(leaf == 2)
    def _():
        move_near.start()

    @pl.when(leaf < 2)
    def _():
        others = coupling(jnp.concatenate([rows_for(3), rows_for(2)], axis=0))
        near, far = others[:PIECE], others[PIECE:]
        mats[1, z, y, c] = near
        mats[2, z, y, c] = jnp.where(leaf == 0, far, near)

    @pl.when(leaf == 0)
    def _():
        move_near.start()

    @pl.when(leaf == 1)
    def _():
        move_far.start()

    loads[2].wait()
    spread(rhs_v[...], packs.at[0], rbuf, 0)

    @pl.when(leaf >= 2)
    def _():
        def strip(r, carry):
            part = pl.ds(pl.multiple_of(r * 256, 256), 256)
            kept = lax.broadcasted_iota(jnp.int32, (256, W), 0) + r * 256 < width
            inv_v[part, :] = jnp.where(kept, inv_v[part, :].astype(F32), 0.0).astype(BF16)
            return carry

        lax.fori_loop(0, 4, strip, 0)

        def column(r, carry):
            part = pl.ds(pl.multiple_of(r * 256, 256), 256)
            gram[:, part] = lax.dot_general(
                inv_v[...], inv_v[:, part], (((0,), (0,)), ((), ())), preferred_element_type=F32
            ).astype(BF16)
            return carry

        lax.fori_loop(0, 4, column, 0)
        move_near.wait_recv()
        gather_first(0)

    gather_second(0)

    @pl.when(leaf == 3)
    def _():
        move_far.wait_recv()

    @pl.when(two_jobs)
    def _():
        gather_first(1)

    gather_third(0)

    @pl.when(two_jobs)
    def _():
        gather_second(1)

    exchange_wait(rbuf, 0)
    state[0] = collect(rbuf)

    gather_last(0)
    gather_wait(0)

    def matrix(j):
        return mats[j].reshape(W, W)

    LOW, HIGH = pl.ds(0, HALF), pl.ds(HALF, HALF)
    halves = (LOW, HIGH)

    def half_rows(j, n):
        return mats[j, 2 * n : 2 * n + 2].reshape(HALF, W)

    def hops(source, target, slot, x):
        return [hop(source.at[:, part], target.at[:, part], slot + n, x) for n, part in enumerate(halves)]

    down = hops(part_out.at[0], part_in.at[0], 0, leaf + 1 - 2 * (leaf // 3))
    pass_on = hops(part_out.at[2], part_in.at[0], 0, 3)
    early = hop(part_out.at[2], part_in.at[1], 2, 2)
    far = hop(part_out.at[1], part_in.at[1], 5, 3)
    skip = hop(part_out.at[2], part_in.at[2], 6, 3)

    def correct(part):
        columns = lax.broadcasted_iota(jnp.int32, (PIECE, HALF), 1) + part.start
        part_out[2, :, part] = jnp.where(columns < width, state[0, :, part], 0.0).astype(BF16)

    @pl.when(leaf == 0)
    def _():
        for part in halves:
            correct(part)
        for n, part in enumerate(halves):
            part_out[0, :, part] = product(part_out[2], half_rows(0, n), True).astype(BF16)
            down[n].start()
        early.start()

    @pl.when(leaf < 2)
    def _():
        gather_first(2)

    @pl.when(leaf == 1)
    def _():
        down[0].wait_recv()
        state[0, :, LOW] = state[0, :, LOW] - part_in[0, :, LOW].astype(F32)
        correct(LOW)
        acc[...] = product(part_out[2, :, LOW], mats[0, :, :, :, :, LOW].reshape(W, HALF), True)
        down[1].wait_recv()
        state[0, :, HIGH] = state[0, :, HIGH] - part_in[0, :, HIGH].astype(F32)
        correct(HIGH)
        for n, part in enumerate(halves):
            rest = product(part_out[2, :, HIGH], mats[0, 2 * n : 2 * n + 2, :, :, :, HIGH].reshape(HALF, HALF), True)
            part_out[0, :, part] = (acc[:, part] + rest).astype(BF16)
            down[n].start()
        skip.start()

    @pl.when(two_jobs)
    def _():
        gather_third(1)

    @pl.when(leaf < 2)
    def _():
        gather_second(2)

    @pl.when(two_jobs)
    def _():
        gather_last(1)
        gather_wait(1)

    @pl.when(leaf == 0)
    def _():
        part_out[1] = product(part_out[2], matrix(1), True).astype(BF16)
        far.start()

    @pl.when(leaf == 2)
    def _():
        early.wait_recv()
        state[0] = state[0] - product(part_in[1], matrix(0), True)
        for n, part in enumerate(halves):
            down[n].wait_recv()
            state[0, :, part] = state[0, :, part] - part_in[0, :, part].astype(F32)
            correct(part)
            pass_on[n].start()

    @pl.when(leaf == 3)
    def _():
        skip.wait_recv()
        state[0] = state[0] - product(part_in[2], matrix(1), True)
        far.wait_recv()
        state[0] = state[0] - part_in[1].astype(F32)
        pass_on[0].wait_recv()
        state[0] = state[0] - product(part_in[0, :, LOW], mats[0, :, :, :, :, LOW].reshape(W, HALF), True)
        pass_on[1].wait_recv()
        state[0] = state[0] - product(part_in[0, :, HIGH], mats[0, :, :, :, :, HIGH].reshape(W, HALF), True)
        for part in halves:
            correct(part)

    ahead = hops(part_out.at[5], part_in.at[5], 14, 3)
    jump = hops(part_out.at[6], part_in.at[3], 8, 1)
    up = hops(part_out.at[4], part_in.at[3], 8, 0)
    last_to_zero = hop(part_out.at[4], part_in.at[4], 10, 0)
    last_to_one = hop(part_out.at[4], part_in.at[4], 12, 1)
    back = hop(part_out.at[6], part_in.at[4], 11, 2)
    across = hop(part_out.at[6], part_in.at[5], 13, 0)

    @pl.when(leaf == 2)
    def _():
        for n, part in enumerate(halves):
            columns = lax.broadcasted_iota(jnp.int32, (PIECE, HALF), 1) + part.start
            own_part = jnp.where(columns < width, product(part_out[2], gram[:, part]), 0.0)
            part_out[5, :, part] = own_part.astype(BF16)
            ahead[n].start()

    @pl.when(leaf == 3)
    def _():
        part_out[4] = jnp.where(live(PIECE), product(part_out[2], gram[...]), 0.0).astype(BF16)
        last_to_one.start()
        for n, part in enumerate(halves):
            term = product(part_out[4], mats[0, :, :, :, :, part].reshape(W, HALF))
            ahead[n].wait_recv()
            part_out[6, :, part] = (part_in[5, :, part].astype(F32) - term).astype(BF16)
            jump[n].start()
        last_to_zero.start()
        across.start()
        back.start()

    forward = jnp.where(live(PIECE), product(part_out[2], inv_v[...], True), 0.0).astype(BF16)

    @pl.when(leaf < 2)
    def _():
        state[1] = jnp.where(live(PIECE), product(forward, inv_v[...]), 0.0)
        gather_third(2)

    spread(forward, packs.at[1], fbuf, 1)

    @pl.when(leaf < 2)
    def _():
        gather_last(2)
        gather_wait(2)

    @pl.when(leaf == 0)
    def _():
        last_to_zero.wait_recv()
        state[1] = state[1] - product(part_in[4], matrix(1))
        across.wait_recv()
        state[1] = state[1] - product(part_in[5], matrix(2))

    @pl.when(leaf == 1)
    def _():
        last_to_one.wait_recv()
        state[1] = state[1] - product(part_in[4], matrix(2))

    @pl.when(leaf < 2)
    def _():
        up[0].wait_recv()
        acc[...] = state[1] - product(part_in[3, :, LOW], half_rows(0, 0))
        up[1].wait_recv()
        for n, part in enumerate(halves):
            term = product(part_in[3, :, HIGH], mats[0, 2:, :, :, :, part].reshape(HALF, HALF))
            part_out[4, :, part] = (acc[:, part] - term).astype(BF16)

            @pl.when(leaf == 1)
            def _():
                up[n].start()

    @pl.when(leaf == 2)
    def _():
        back.wait_recv()
        part_out[4] = part_in[4]

    spread(part_out[4], packs.at[2], obuf, 2)

    exchange_wait(fbuf, 1)
    fwd_o[...] = collect(fbuf).astype(BF16)

    gather_sent(0)

    @pl.when(two_jobs)
    def _():
        gather_sent(1)

    @pl.when(leaf < 2)
    def _():
        gather_sent(2)

    def sent(when, copies):
        @pl.when(when)
        def _():
            for copy in copies:
                copy.wait_send()

    sent(leaf == 0, [move_near, *down, early, far])
    sent(leaf == 1, [move_far, *down, skip, *up])
    sent(leaf == 2, [move_near, *pass_on, *ahead])
    sent(leaf == 3, [last_to_one, *jump, last_to_zero, across, back])

    exchange_wait(obuf, 2)
    sol_o[...] = collect(obuf).astype(BF16)


def local(rhs, inverse_blocks, update_blocks, targets, widths):
    hbm = pl.BlockSpec(memory_space=pltpu.HBM)
    vmem = pl.BlockSpec(memory_space=pltpu.VMEM)
    dma = pltpu.SemaphoreType.DMA
    forward, solved = pl.pallas_call(
        kernel,
        out_shape=(jax.ShapeDtypeStruct((PIECE, W), BF16),) * 2,
        in_specs=[hbm] * 5,
        out_specs=(vmem, vmem),
        scratch_shapes=[
            pltpu.VMEM((PIECE, W), BF16),
            pltpu.VMEM((W, W), BF16),
            pltpu.VMEM((SLOTS, PIECE, W), BF16),
            pltpu.SMEM((SLOTS,), jnp.int32),
            pltpu.SMEM((1,), jnp.int32),
            pltpu.VMEM((W, W), BF16),
            pltpu.VMEM((3, LINE, LINE, 2, PIECE, W), BF16),
            pltpu.VMEM((GRID, 16, 128), BF16),
            pltpu.VMEM((GRID, 16, 128), BF16),
            pltpu.VMEM((GRID, 16, 128), BF16),
            pltpu.VMEM((3, 2, 16, W), BF16),
            pltpu.VMEM((7, PIECE, W), BF16),
            pltpu.VMEM((6, PIECE, W), BF16),
            pltpu.VMEM((2, PIECE, W), F32),
            pltpu.VMEM((PIECE, W), F32),
            dma((8,)),
            dma((3, 2, 6)),
            dma((3, 2, 28)),
            dma((3,)),
            dma((3,)),
            dma((16,)),
            dma((16,)),
        ],
        compiler_params=pltpu.CompilerParams(
            collective_id=0, has_side_effects=True, vmem_limit_bytes=55040 << 10
        ),
        name="solve",
    )(rhs[0], inverse_blocks[0], update_blocks[0], targets[0, :, 0], widths)
    return forward[None], solved[None]


def solution(mesh):
    placed = (
        P("leaf", "grid", None),
        P("leaf", None, None),
        P("leaf", None, "grid", None),
        P("leaf", None, "grid"),
        P("leaf"),
    )
    return jax.shard_map(
        local,
        mesh=mesh,
        in_specs=placed,
        out_specs=(P("leaf", "grid", None), P("leaf", "grid", None)),
        check_vma=False,
    )
```
